256 devices in a mesh: band: 4 (over x), py: 4 (over z_hi), pz: 16 (over z_lo, y, core).
Axes of the slice: x: 4, y: 4, z: 8 (z_hi: 4, z_lo: 2; z = z_hi * 2 + z_lo), core: 2. Of those that a mesh axis runs over, the one named last changes fastest.
Arguments:
- coefficients: float32 [8, 256, 256, 256], P('band', 'pz', 'py'), parts along dimension 0, may hold values from -6 to 6
- potential: float32 [256, 256, 256], P('pz', 'py'), may hold values from -6 to 6
- column_limit: int32 [256, 256], P('pz', 'py'), may hold values from -1 to 96, as said below
- entry_atom: int32 [32768, 1], P(('py', 'pz')), may hold values from 0 to 4095, as said below
- entry_block: int32 [32768], P(('py', 'pz')), may hold values from 0 to 2047, as said below
- projectors: float32 [32768, 8, 128], P(('py', 'pz')), may hold values from -0.6 to 0.6
- coupling: float32 [8, 8], replicated, may hold values from -4 to 4
Outputs:
- applied: float32 [8, 256, 256, 256], P('band', 'pz', 'py'), parts along dimension 0
The draws below stay inside these ranges and needn't reach their ends.
There are 4 independent parts, one for each index of `band`. The reference program is written for one: setup_inputs(seed, part) draws one part's arguments, and reference() takes and returns one part's arrays. A program takes and returns all parts, laid end to end along the dimension named above; an argument that names none is the same for every part. Nothing has to cross between parts.
Inputs may be any that keep to these rules, and one draw needn't show every extreme that they name: column_limit[y, x] = (number of k in 0..128 with k^2 + freq(y)^2 + freq(x)^2 + j <= 96^2) - 1, with j in 0..2 drawn for each column and 0 at column (0, 0); -1 marks an empty column. `entry_atom`: atom a is centred on device a // (4096 / (4 * 16)); an entry of device (p, q) names an atom centred on (p, q) or on one of its four neighbours (p - 1, q), (p + 1, q), (p, q - 1), (p, q + 1), indices taken modulo 4 and 16; the first 4096 / (4 * 16) entries of each device name its own atoms in order. `entry_block`: the blocks of one atom's entries lie within four blocks of one centre block of that atom, modulo 2048.
All inputs are finite; a program needn't handle non-finite values.
Results may differ from the reference program's by a relative error of at most 0.00007.
Values sent between devices are 32-bit elements; how exact they have to be, the bound alone decides.
A program may use at most 128 MiB of HBM per device.

```python
import math
import jax
import jax.numpy as jnp
from jax import lax

GRID = 256
NB = 2
NPROJ = 8
BLOCK = 128
NATOM = 4096
E_DEV = 512
ENTRIES = 32768
NBLK = 2048
N_PY = 4
N_PZ = 16


def draw_column_limit(key, part):
    key = jax.random.fold_in(key, 11)
    jitter = jax.random.randint(key, (GRID, GRID), 0, 3)
    indices = jnp.arange(GRID, dtype=jnp.int32)
    freqs = jnp.minimum(indices, GRID - indices)
    anchor = (indices[:, None] == 0) & (indices[None, :] == 0)
    base = freqs[:, None] ** 2 + freqs[None, :] ** 2 + jnp.where(anchor, 0, jitter)
    radius = 3 * GRID // 8
    depth_freq = jnp.arange(GRID // 2 + 1, dtype=jnp.int32)
    inside = depth_freq[:, None, None] ** 2 + base[None, :, :] <= radius * radius
    counted = jnp.sum(inside.astype(jnp.int32), axis=0)
    return (counted - 1).astype(jnp.int32)


def entry_layout(key):
    base_key = jax.random.fold_in(key, 101)
    side_key, local_key, centre_key, offset_key = jax.random.split(base_key, 4)
    per_device = NATOM // (N_PY * N_PZ)
    ids = jnp.arange(ENTRIES, dtype=jnp.int32)
    device = ids // E_DEV
    within = ids % E_DEV
    row_index = device // N_PZ
    col_index = device % N_PZ
    side = jax.random.randint(side_key, (ENTRIES,), 0, 8)
    near_row = jnp.where(side == 4, (row_index - 1) % N_PY, jnp.where(side == 5, (row_index + 1) % N_PY, row_index))
    near_col = jnp.where(side == 6, (col_index - 1) % N_PZ, jnp.where(side == 7, (col_index + 1) % N_PZ, col_index))
    local_atom = jax.random.randint(local_key, (ENTRIES,), 0, per_device)
    own_first = within < per_device
    near_row = jnp.where(own_first, row_index, near_row)
    near_col = jnp.where(own_first, col_index, near_col)
    local_atom = jnp.where(own_first, within, local_atom)
    atoms = ((near_row * N_PZ + near_col) * per_device + local_atom).astype(jnp.int32)
    centre = jax.random.randint(centre_key, (NATOM,), 0, NBLK)
    centre = centre.at[0].set(NBLK - 1).at[1 % NATOM].set(0)
    offset = jax.random.randint(offset_key, (ENTRIES,), 0, 4)
    offset = jnp.where(own_first, 0, offset)
    blocks = ((centre[atoms] + offset) % NBLK).astype(jnp.int32)
    return (atoms, blocks)


def draw_entry_atom(key, part):
    atoms, blocks = entry_layout(key)
    return atoms[:, None].astype(jnp.int32)


def draw_entry_block(key, part):
    atoms, blocks = entry_layout(key)
    return blocks.astype(jnp.int32)


def shard_levels(key, dims, cuts, low, largest):
    def one(dim, blocks):
        heights = jax.random.uniform(jax.random.fold_in(jax.random.fold_in(key, 6), dim), (blocks,), jnp.float32, low / len(cuts), largest / len(cuts))
        return jnp.repeat(jnp.exp(heights), dims[dim] // blocks).reshape((-1,) + (1,) * (len(dims) - dim - 1))

    gain = one(*cuts[0])
    for cut in cuts[1:]:
        gain = gain * one(*cut)
    return gain


def gaussian(rng, dims, deviation, reach, pieces=(), kind=jnp.bfloat16):
    entries = deviation * jax.random.normal(rng, dims, jnp.float32)
    if pieces:
        entries = entries * shard_levels(rng, dims, pieces, -0.22, 0.18)
    return jnp.clip(entries, -reach, reach).astype(kind)


def setup_inputs(seed: int = 0, part: int = 0) -> dict:
    key_list = jax.random.split(jax.random.key(seed), 8)
    own_keys = jax.random.split(jax.random.fold_in(key_list[7], part), 8)
    return {
        "coefficients": gaussian(own_keys[0], (NB, GRID, GRID, GRID), 1.0, 6.0, ((1, 16), (2, 4)), jnp.float32),
        "potential": gaussian(key_list[1], (GRID, GRID, GRID), 1.0, 6.0, ((0, 16), (1, 4)), jnp.float32),
        "column_limit": draw_column_limit(jax.random.fold_in(key_list[7], 71), part),
        "entry_atom": draw_entry_atom(jax.random.fold_in(key_list[7], 71), part),
        "entry_block": draw_entry_block(jax.random.fold_in(key_list[7], 71), part),
        "projectors": gaussian(key_list[5], (ENTRIES, NPROJ, BLOCK), 0.1, 0.6, ((0, 64),), jnp.float32),
        "coupling": gaussian(key_list[6], (NPROJ, NPROJ), 1.0, 4.0, (), jnp.float32),
    }


HIGHEST_MODE = lax.Precision.HIGHEST

def cas_table(points):
    indices = jnp.arange(points, dtype=jnp.int32)
    product = indices[:, None] * indices[None, :] % points
    angles = product.astype(jnp.float32) * (2.0 * math.pi / points)
    return (jnp.cos(angles) + jnp.sin(angles)) / math.sqrt(points)

def frequency(indices, points):
    return jnp.minimum(indices, points - indices)

def along_depth(hartley, values):
    return jnp.einsum('ka,nayx->nkyx', hartley, values, precision=HIGHEST_MODE)

def along_rows(hartley, values):
    return jnp.einsum('ka,nzax->nzkx', hartley, values, precision=HIGHEST_MODE)

def along_width(hartley, values):
    return jnp.einsum('ka,nzya->nzyk', hartley, values, precision=HIGHEST_MODE)

def reference(coefficients, potential, column_limit, entry_atom, entry_block, projectors, coupling):
    hartley = cas_table(GRID)
    freqs = frequency(jnp.arange(GRID, dtype=jnp.int32), GRID)
    sphere = (freqs[None, None, :] <= column_limit[:, :, None]).astype(jnp.float32)
    squared = freqs[:, None, None] ** 2 + freqs[None, :, None] ** 2 + freqs[None, None, :] ** 2
    kinetic = 0.5 * squared.astype(jnp.float32) * (4.0 / GRID) ** 2
    masked = coefficients * sphere[None]
    start = jnp.transpose(masked, (0, 3, 1, 2))
    real_field = along_width(hartley, along_rows(hartley, along_depth(hartley, start)))
    depth_local = GRID // N_PZ
    rows_local = GRID // N_PY
    devices_all = N_PY * N_PZ
    blocks = real_field.reshape(NB, N_PZ, depth_local, N_PY, rows_local, GRID)
    blocks = blocks.transpose(3, 1, 0, 2, 4, 5).reshape(devices_all, NB, NBLK, BLOCK)
    owner = jnp.arange(ENTRIES, dtype=jnp.int32) // E_DEV
    gathered = blocks[owner, :, entry_block]
    partial_terms = jnp.einsum('epc,enc->epn', projectors, gathered, precision=HIGHEST_MODE)
    atom_terms = jax.ops.segment_sum(partial_terms, entry_atom[:, 0], num_segments=NATOM)
    symmetric = 0.5 * (coupling + coupling.T)
    coupled = jnp.einsum('qp,apn->aqn', symmetric, atom_terms, precision=HIGHEST_MODE)
    selected = coupled[entry_atom[:, 0]]
    spread = jnp.einsum('epc,epn->enc', projectors, selected, precision=HIGHEST_MODE)
    target = owner * NBLK + entry_block
    placed = jax.ops.segment_sum(spread, target, num_segments=devices_all * NBLK)
    placed = placed.reshape(N_PY, N_PZ, NBLK, NB, BLOCK).transpose(3, 0, 1, 2, 4)
    placed = placed.reshape(NB, N_PY, N_PZ, depth_local, rows_local, GRID)
    projected = placed.transpose(0, 2, 3, 1, 4, 5).reshape(NB, GRID, GRID, GRID)
    total = potential[None] * real_field + projected
    back = along_depth(hartley, along_rows(hartley, along_width(hartley, total)))
    back = jnp.transpose(back, (0, 2, 3, 1))
    return sphere[None] * (kinetic[None] * masked + back)
```

```python
import functools
import math

import jax
import jax.numpy as jnp
import numpy as np
from jax import lax
from jax.experimental import pallas as pl
from jax.experimental.pallas import tpu as pltpu
from jax.sharding import PartitionSpec as P

F32 = jnp.float32
BF16 = jnp.bfloat16
I32 = jnp.int32
MESH = pl.DeviceIdType.MESH
HIGHEST = lax.Precision.HIGHEST

NPY, NPZ = 4, 16
GRID = 256
CHUNKS = 4
ZC = 16 // CHUNKS
ENT = 512
OPPOSITE = (0, 2, 1, 4, 3)


def cas_matrix():
    index = np.arange(GRID)
    angle = (index[:, None] * index[None, :] % GRID) * (2.0 * math.pi / GRID)
    return ((np.cos(angle) + np.sin(angle)) / math.sqrt(GRID)).astype(np.float32)


def halves(table):
    high = table.astype(jnp.bfloat16)
    low = (table - high.astype(np.float32)).astype(jnp.bfloat16)
    return high, low


def tables():
    cas = cas_matrix()
    wide = np.zeros((4, 2, 64, 2, GRID), np.float32)
    for band in range(2):
        wide[:, band, :, band, :] = cas.reshape(4, 64, GRID)
    wide = wide.reshape(512, 512)
    return halves(cas) + halves(wide) + halves(np.ascontiguousarray(wide.T))


def split(values):
    high = values.astype(BF16)
    return high, (values - high.astype(F32)).astype(BF16)


NN = (((1,), (0,)), ((), ()))
NT = (((1,), (1,)), ((), ()))
TN = (((0,), (0,)), ((), ()))


def mm(a, b, dims=NN):
    return lax.dot_general(a, b, dims, preferred_element_type=F32)


def mm3(a, b, dims=NN):
    (a_high, a_low), (b_high, b_low) = a, b
    return mm(a_high, b_high, dims) + (mm(a_high, b_low, dims) + mm(a_low, b_high, dims))


def iota(shape, dim):
    return lax.broadcasted_iota(I32, shape, dim)


def freq(index):
    return jnp.minimum(index, GRID - index)


def kernel(
    coef, limit, atom, block, coupling, chi, clo, pot_any, proj_any, whi_any, wlo_any, vhi_any, vlo_any,
    out,
    pot, proj, whi, wlo, vhi, vlo,
    zt, got1, yt, got2, field, xb, got3, yb, got4,
    rows_hot, cols_hot, parity, atom_hot, gathered, spread_hi, spread_lo, terms, terms_in, coupled,
    local_sem, s1, r1, s2, r2, s3, r3, s4, r4, st, rt, sc, rc,
):
    p = lax.axis_index("py")
    q = lax.axis_index("pz")
    full = jnp.logical_or(q < 6, q > 9)

    loads = [
        pltpu.make_async_copy(src, dst, local_sem.at[k])
        for k, (src, dst) in enumerate(
            [(whi_any, whi), (wlo_any, wlo), (proj_any, proj), (pot_any, pot), (vhi_any, vhi), (vlo_any, vlo)]
        )
    ]
    for load in loads:
        load.start()

    got1[:, 96:160, :] = jnp.zeros((16, 64, 128), F32)

    barrier = pltpu.get_barrier_semaphore()
    for o in range(1, NPZ):
        pl.semaphore_signal(barrier, inc=1, device_id={"pz": lax.rem(q + o, NPZ)}, device_id_type=MESH)
    for o in range(1, NPY):
        pl.semaphore_signal(barrier, inc=1, device_id={"py": lax.rem(p + o, NPY)}, device_id_type=MESH)

    c_pair = (chi[...], clo[...])

    def inside(y):
        row = limit[pl.ds(y, 1), :].astype(F32)
        diag = jnp.where(iota((64, 64), 0) == iota((64, 64), 1), jnp.broadcast_to(row, (64, 64)), 0.0)
        bound = mm(diag.astype(BF16), jnp.ones((64, GRID), BF16))
        return freq(iota((64, GRID), 1)).astype(F32) <= bound

    zt_rows = zt.reshape(4096, 128)

    def depth_step(y, carry):
        keep = inside(y)
        pair = jnp.concatenate([jnp.where(keep, coef[0, y], 0.0), jnp.where(keep, coef[1, y], 0.0)], axis=0)
        zt_rows[pl.ds(y, GRID, stride=16), :] = mm3(c_pair, split(pair), NT)
        return carry

    lax.fori_loop(0, 16, depth_step, 0)

    pl.semaphore_wait(barrier, NPZ + NPY - 2)

    def copy1(c, t, src_q, height):
        return pltpu.make_async_remote_copy(
            src_ref=zt.at[pl.ds(16 * t + ZC * c, ZC), pl.ds(0, height), :],
            dst_ref=got1.at[pl.ds(ZC * c, ZC), pl.ds(pl.multiple_of(16 * src_q, 16), height), :],
            send_sem=s1.at[c, t],
            recv_sem=r1.at[c, src_q],
            device_id={"pz": t},
            device_id_type=MESH,
        )

    def each_peer(action):
        def step(o, carry):
            action(lax.rem(q + o, NPZ))
            return carry

        lax.fori_loop(1, NPZ, step, 0)

    def ends1(c, action):
        @pl.when(full)
        def _():
            each_peer(lambda t: action(copy1(c, t, q, 16)))

        @pl.when(q == 6)
        def _():
            each_peer(lambda t: action(copy1(c, t, q, 8)))

    for c in range(CHUNKS):
        ends1(c, lambda copy: copy.start())
    got1[:, pl.ds(pl.multiple_of(16 * q, 16), 16), :] = zt[pl.ds(16 * q, 16), :, :]

    def wait1(c):
        def step(o, carry):
            t = lax.rem(q + o, NPZ)

            @pl.when(jnp.logical_or(t < 6, t > 9))
            def _():
                copy1(c, q, t, 16).wait_recv()

            @pl.when(t == 6)
            def _():
                copy1(c, q, t, 8).wait_recv()

            return carry

        lax.fori_loop(1, NPZ, step, 0)

    block_row = block[...]
    row_of = lax.shift_right_logical(block_row, 1)
    for k in range(8):
        hot = iota((128, ENT), 0) + 128 * k == jnp.broadcast_to(row_of, (128, ENT))
        rows_hot[128 * k : 128 * k + 128, :] = jnp.where(hot, 1.0, 0.0).astype(BF16)

    eye = iota((ENT, ENT), 0) == iota((ENT, ENT), 1)

    def to_column(row):
        diag = jnp.where(eye, jnp.broadcast_to(row.astype(F32), (ENT, ENT)), 0.0)
        return mm(diag.astype(BF16), jnp.ones((ENT, 128), BF16))

    row_col = 32.0 * to_column(lax.shift_right_logical(row_of, 5)) + to_column(row_of & 31)
    for k in range(8):
        hot = (iota((ENT, 128), 1) + 128 * k).astype(F32) == row_col
        cols_hot[:, 128 * k : 128 * k + 128] = jnp.where(hot, 1.0, 0.0).astype(BF16)
    parity[...] = to_column(block_row & 1)

    atoms = atom[...]
    owner = lax.shift_right_logical(atoms, 6)
    dp = (lax.shift_right_logical(owner, 4) - p) & 3
    dq = ((owner & 15) - q) & 15
    slot = jnp.where(dp == 3, 1, jnp.where(dp == 1, 2, jnp.where(dq == 15, 3, jnp.where(dq == 1, 4, 0))))
    code = slot * 64 + (atoms & 63)
    hot = iota((320, ENT), 0) == jnp.broadcast_to(code, (320, ENT))
    atom_hot[...] = jnp.where(hot, 1.0, 0.0).astype(BF16)

    def rows_pass(c, src, dst):
        def step(i, carry):
            z = ZC * c + 2 * i
            both = jnp.concatenate([src[z], src[z + 1]], axis=1)
            done = mm3(c_pair, split(both))
            dst[z] = done[:, :128]
            dst[z + 1] = done[:, 128:]
            return carry

        lax.fori_loop(0, ZC // 2, step, 0)

    def copy2(c, t, src_p):
        return pltpu.make_async_remote_copy(
            src_ref=yt.at[pl.ds(ZC * c, ZC), pl.ds(pl.multiple_of(64 * t, 64), 64), :],
            dst_ref=got2.at[src_p, pl.ds(ZC * c, ZC), :, :],
            send_sem=s2.at[c, t],
            recv_sem=r2.at[c, src_p],
            device_id={"py": t},
            device_id_type=MESH,
        )

    for c in range(CHUNKS):
        wait1(c)
        rows_pass(c, got1, yt)
        for o in (2, 1, 3):
            copy2(c, lax.rem(p + o, NPY), p).start()
        got2[p, ZC * c : ZC * c + ZC] = yt[ZC * c : ZC * c + ZC, pl.ds(pl.multiple_of(64 * p, 64), 64), :]

    loads[0].wait()
    loads[1].wait()
    height = 64 * ZC
    w_pair = (whi[...], wlo[...])
    for c in range(CHUNKS):
        for o in range(1, NPY):
            copy2(c, p, lax.rem(p + o, NPY)).wait_recv()
        lines = jnp.concatenate([got2[k, ZC * c : ZC * c + ZC].reshape(height, 128) for k in range(NPY)], axis=1)
        real = mm3(split(lines), w_pair)
        field[height * c : height * c + height, :] = real
        high, low = split(real)
        hot = cols_hot[:, height * c : height * c + height]
        part = mm(hot, high) + mm(hot, low)
        if c == 0:
            gathered[...] = part
        else:
            gathered[...] += part

    loads[2].wait()
    proj_rows = proj.reshape(ENT * 8, 128)
    odd = parity[...] > 0.5
    lane = iota((256, 128), 1)
    entry_terms = jnp.zeros((ENT, 128), F32)
    for n in range(2):
        cells = jnp.where(odd, gathered[:, 256 * n + 128 : 256 * n + 256], gathered[:, 256 * n : 256 * n + 128])
        for i in range(8):
            high, low = split(proj_rows[pl.ds(i, ENT, stride=8), :] * cells)
            column = jnp.where(lane == 8 * n + i, 1.0, 0.0).astype(BF16)
            entry_terms += mm(jnp.concatenate([high, low], axis=1), column)
    high, low = split(entry_terms)
    hot = atom_hot[...]
    terms[...] = (mm(hot, high) + mm(hot, low)).reshape(5, 64, 128)

    def neighbour(s):
        if s < 3:
            return {"py": lax.rem(p + (3 if s == 1 else 1), NPY)}
        return {"pz": lax.rem(q + (15 if s == 3 else 1), NPZ)}

    def copy_terms(s):
        return pltpu.make_async_remote_copy(
            src_ref=terms.at[s], dst_ref=terms_in.at[OPPOSITE[s]], send_sem=st.at[s], recv_sem=rt.at[OPPOSITE[s]],
            device_id=neighbour(s), device_id_type=MESH,
        )

    def copy_coupled(s):
        return pltpu.make_async_remote_copy(
            src_ref=coupled.at[0], dst_ref=coupled.at[OPPOSITE[s]], send_sem=sc.at[s], recv_sem=rc.at[OPPOSITE[s]],
            device_id=neighbour(s), device_id_type=MESH,
        )

    for s in range(1, 5):
        copy_terms(s).start()
    symmetric = 0.5 * (coupling[...] + coupling[...].T)
    place = jnp.where((iota((128, 8), 0) & 7) == iota((128, 8), 1), 1.0, 0.0)
    tiled = jnp.dot(jnp.dot(place, symmetric, precision=HIGHEST), place.T, precision=HIGHEST)
    same = lax.shift_right_logical(iota((128, 128), 0), 3) == lax.shift_right_logical(iota((128, 128), 1), 3)
    mix = jnp.where(same, tiled, 0.0)
    total = terms[0]
    for s in range(1, 5):
        copy_terms(OPPOSITE[s]).wait_recv()
        total = total + terms_in[s]
    coupled[0] = jnp.dot(total, mix, precision=HIGHEST)
    for s in range(1, 5):
        copy_coupled(s).start()
    for s in range(1, 5):
        copy_coupled(OPPOSITE[s]).wait_recv()
    high, low = split(coupled[...].reshape(320, 128))
    chosen = mm(hot, high, TN) + mm(hot, low, TN)
    for n in range(2):
        cells = jnp.zeros((ENT, 128), F32)
        for i in range(8):
            j = 8 * n + i
            weight = jnp.broadcast_to(chosen[:, j : j + 1], (ENT, 128))
            cells += proj_rows[pl.ds(i, ENT, stride=8), :] * weight
        high, low = split(cells)
        zero = jnp.zeros_like(high)
        keep = odd.astype(F32).astype(BF16) > 0.5
        spread_hi[:, 256 * n : 256 * n + 128] = jnp.where(keep, zero, high)
        spread_hi[:, 256 * n + 128 : 256 * n + 256] = jnp.where(keep, high, zero)
        spread_lo[:, 256 * n : 256 * n + 128] = jnp.where(keep, zero, low)
        spread_lo[:, 256 * n + 128 : 256 * n + 256] = jnp.where(keep, low, zero)

    def copy3(c, t, src_p):
        return pltpu.make_async_remote_copy(
            src_ref=xb.at[t, pl.ds(ZC * c, ZC), :, :],
            dst_ref=got3.at[pl.ds(ZC * c, ZC), pl.ds(pl.multiple_of(64 * src_p, 64), 64), :],
            send_sem=s3.at[c, t],
            recv_sem=r3.at[c, src_p],
            device_id={"py": t},
            device_id_type=MESH,
        )

    loads[3].wait()
    loads[4].wait()
    loads[5].wait()
    v_pair = (vhi[...], vlo[...])
    for c in range(CHUNKS):
        rows = slice(height * c, height * c + height)
        hot = rows_hot[rows, :]
        placed = mm(hot, spread_hi[...]) + mm(hot, spread_lo[...])
        local = pot[ZC * c : ZC * c + ZC].reshape(height, GRID)
        whole = jnp.concatenate([local, local], axis=1) * field[rows, :] + placed
        done = mm3(split(whole), v_pair)
        for k in range(NPY):
            xb[k, ZC * c : ZC * c + ZC] = done[:, 128 * k : 128 * k + 128].reshape(ZC, 64, 128)
        for o in (2, 1, 3):
            copy3(c, lax.rem(p + o, NPY), p).start()
        got3[ZC * c : ZC * c + ZC, pl.ds(pl.multiple_of(64 * p, 64), 64), :] = xb[p, ZC * c : ZC * c + ZC]

    def copy4(c, t, src_q, height):
        return pltpu.make_async_remote_copy(
            src_ref=yb.at[pl.ds(ZC * c, ZC), pl.ds(pl.multiple_of(16 * t, 16), height), :],
            dst_ref=got4.at[pl.ds(16 * src_q + ZC * c, ZC), pl.ds(0, height), :],
            send_sem=s4.at[c, t],
            recv_sem=r4.at[c, src_q],
            device_id={"pz": t},
            device_id_type=MESH,
        )

    def ends4(c, action):
        def one(t):
            @pl.when(jnp.logical_or(t < 6, t > 9))
            def _():
                action(copy4(c, t, q, 16))

            @pl.when(t == 6)
            def _():
                action(copy4(c, t, q, 8))

        each_peer(one)

    for c in range(CHUNKS):
        for o in range(1, NPY):
            copy3(c, p, lax.rem(p + o, NPY)).wait_recv()
        rows_pass(c, got3, yb)
        ends4(c, lambda copy: copy.start())
    got4[pl.ds(16 * q, 16), :, :] = yb[:, pl.ds(pl.multiple_of(16 * q, 16), 16), :]
    for c in range(CHUNKS):

        @pl.when(full)
        def _():
            each_peer(lambda t: copy4(c, q, t, 16).wait_recv())

        @pl.when(q == 6)
        def _():
            each_peer(lambda t: copy4(c, q, t, 8).wait_recv())

    got4_rows = got4.reshape(4096, 128)

    def final_step(y, carry):
        keep = inside(y)
        lines = got4_rows[pl.ds(y, GRID, stride=16), :]
        done = mm3(split(lines), c_pair, TN)
        fy = freq(16 * q + y)
        fx = freq(64 * p + iota((64, GRID), 0))
        fz = freq(iota((64, GRID), 1))
        kinetic = (fz * fz + fx * fx + fy * fy).astype(F32) * (0.5 * (4.0 / GRID) ** 2)
        for n in range(2):
            out[n, y] = jnp.where(keep, kinetic * coef[n, y] + done[64 * n : 64 * n + 64, :], 0.0)
        return carry

    lax.fori_loop(0, 16, final_step, 0)

    for c in range(CHUNKS):
        ends1(c, lambda copy: copy.wait_send())
        ends4(c, lambda copy: copy.wait_send())
        for o in range(1, NPY):
            t = lax.rem(p + o, NPY)
            copy2(c, t, p).wait_send()
            copy3(c, t, p).wait_send()
    for s in range(1, 5):
        copy_terms(s).wait_send()
        copy_coupled(s).wait_send()


def shards(coefficients, potential, column_limit, entry_atom, entry_block, projectors, coupling):
    vmem = pl.BlockSpec(memory_space=pltpu.VMEM)
    anywhere = pl.BlockSpec(memory_space=pl.ANY)
    big = pltpu.VMEM((16, 256, 128), F32)
    dma = pltpu.SemaphoreType.DMA
    return pl.pallas_call(
        kernel,
        name="hamiltonian",
        out_shape=jax.ShapeDtypeStruct(coefficients.shape, F32),
        in_specs=[vmem] * 7 + [anywhere] * 6,
        out_specs=vmem,
        scratch_shapes=[
            pltpu.VMEM((16, 64, GRID), F32),
            pltpu.VMEM((ENT, 8, 128), F32),
            pltpu.VMEM((512, 512), BF16),
            pltpu.VMEM((512, 512), BF16),
            pltpu.VMEM((512, 512), BF16),
            pltpu.VMEM((512, 512), BF16),
            pltpu.VMEM((256, 16, 128), F32),
            big,
            big,
            pltpu.VMEM((NPY, 16, 64, 128), F32),
            pltpu.VMEM((1024, 512), F32),
            pltpu.VMEM((NPY, 16, 64, 128), F32),
            big,
            big,
            pltpu.VMEM((256, 16, 128), F32),
            pltpu.VMEM((1024, ENT), BF16),
            pltpu.VMEM((ENT, 1024), BF16),
            pltpu.VMEM((ENT, 128), F32),
            pltpu.VMEM((320, ENT), BF16),
            pltpu.VMEM((ENT, 512), F32),
            pltpu.VMEM((ENT, 512), BF16),
            pltpu.VMEM((ENT, 512), BF16),
            pltpu.VMEM((5, 64, 128), F32),
            pltpu.VMEM((5, 64, 128), F32),
            pltpu.VMEM((5, 64, 128), F32),
            dma((6,)),
            dma((CHUNKS, NPZ)),
            dma((CHUNKS, NPZ)),
            dma((CHUNKS, NPY)),
            dma((CHUNKS, NPY)),
            dma((CHUNKS, NPY)),
            dma((CHUNKS, NPY)),
            dma((CHUNKS, NPZ)),
            dma((CHUNKS, NPZ)),
            dma((5,)),
            dma((5,)),
            dma((5,)),
            dma((5,)),
        ],
        compiler_params=pltpu.CompilerParams(
            collective_id=0, has_side_effects=True, vmem_limit_bytes=56 * 2**20
        ),
    )(
        coefficients,
        column_limit,
        entry_atom.reshape(1, ENT),
        entry_block.reshape(1, ENT),
        coupling,
        *(jnp.asarray(t) for t in tables()[:2]),
        potential,
        projectors,
        *(jnp.asarray(t) for t in tables()[2:]),
    )


def solution(mesh):
    in_specs = (
        P("band", "pz", "py", None),
        P("pz", "py", None),
        P("pz", "py"),
        P(("py", "pz"), None),
        P(("py", "pz")),
        P(("py", "pz"), None, None),
        P(),
    )
    out_specs = P("band", "pz", "py", None)
    return jax.shard_map(shards, mesh=mesh, in_specs=in_specs, out_specs=out_specs, check_vma=False)
```

```python
import functools
import math

import jax
import jax.numpy as jnp
import numpy as np
from jax import lax
from jax.experimental import pallas as pl
from jax.experimental.pallas import tpu as pltpu
from jax.sharding import PartitionSpec as P

F32 = jnp.float32
BF16 = jnp.bfloat16
I32 = jnp.int32
MESH = pl.DeviceIdType.MESH
HIGHEST = lax.Precision.HIGHEST

NPY, NPZ = 4, 16
GRID = 256
CHUNKS = 8
ZC = 2
ROWS = 64 * ZC
ENT = 512
OPPOSITE = (0, 2, 1, 4, 3)


def cas_matrix():
    index = np.arange(GRID)
    angle = (index[:, None] * index[None, :] % GRID) * (2.0 * math.pi / GRID)
    return ((np.cos(angle) + np.sin(angle)) / math.sqrt(GRID)).astype(np.float32)


def halves(table):
    high = table.astype(jnp.bfloat16)
    low = (table - high.astype(np.float32)).astype(jnp.bfloat16)
    return high, low


def split(values):
    high = values.astype(BF16)
    return high, (values - high.astype(F32)).astype(BF16)


NN = (((1,), (0,)), ((), ()))
NT = (((1,), (1,)), ((), ()))
TN = (((0,), (0,)), ((), ()))


def mm(a, b, dims=NN):
    return lax.dot_general(a, b, dims, preferred_element_type=F32)


def mm3(a, b, dims=NN):
    (a_high, a_low), (b_high, b_low) = a, b
    return mm(a_high, b_high, dims) + (mm(a_high, b_low, dims) + mm(a_low, b_high, dims))


def iota(shape, dim):
    return lax.broadcasted_iota(I32, shape, dim)


def freq(index):
    return jnp.minimum(index, GRID - index)


def kernel(
    limit, atom, block, coupling, chi, clo, coef_any, pot_any, proj_any,
    out_any,
    coef, pot, proj, result,
    zt, got1, yt, got2, field, xb, got3, yb, got4,
    rows_hot, cols_hot, parity, atom_hot, gathered, spread_hi, spread_lo, terms, terms_in, coupled,
    local_sem, coef_sem, out_sem, send_sem, r1, r2, r3, r4, st, rt, sc, rc,
):
    p = lax.axis_index("py")
    q = lax.axis_index("pz")
    full = jnp.logical_or(q < 6, q > 9)

    coef_loads = [
        pltpu.make_async_copy(coef_any.at[:, 4 * k : 4 * k + 4], coef.at[:, 4 * k : 4 * k + 4], coef_sem.at[k])
        for k in range(4)
    ]
    loads = [
        pltpu.make_async_copy(proj_any, proj, local_sem.at[0]),
        pltpu.make_async_copy(pot_any, pot, local_sem.at[1]),
    ]
    for load in coef_loads + loads:
        load.start()

    got1[:, 96:160, :] = jnp.zeros((16, 64, 128), F32)

    barrier = pltpu.get_barrier_semaphore()
    for o in range(1, NPZ):
        pl.semaphore_signal(barrier, inc=1, device_id={"pz": lax.rem(q + o, NPZ)}, device_id_type=MESH)
    for o in range(1, NPY):
        pl.semaphore_signal(barrier, inc=1, device_id={"py": lax.rem(p + o, NPY)}, device_id_type=MESH)

    def table():
        return chi[...], clo[...]

    def apart(work):
        pl.when(q >= 0)(work)

    def inside(y):
        row = limit[pl.ds(y, 1), :].astype(F32)
        diag = jnp.where(iota((64, 64), 0) == iota((64, 64), 1), jnp.broadcast_to(row, (64, 64)), 0.0)
        bound = mm(diag.astype(BF16), jnp.ones((64, GRID), BF16))
        return freq(iota((64, GRID), 1)).astype(F32) <= bound

    zt_rows = zt.reshape(4096, 128)

    def depth_step(y, carry):
        keep = inside(y)
        pair = jnp.concatenate([jnp.where(keep, coef[0, y], 0.0), jnp.where(keep, coef[1, y], 0.0)], axis=0)
        zt_rows[pl.ds(y, GRID, stride=16), :] = mm3(table(), split(pair), NT)
        return carry

    for k in range(4):
        coef_loads[k].wait()
        lax.fori_loop(4 * k, 4 * k + 4, depth_step, 0, unroll=4)

    pl.semaphore_wait(barrier, NPZ + NPY - 2)

    def arrived(buffer, units, semaphore):
        pltpu.make_async_remote_copy(
            src_ref=buffer.at[pl.ds(0, units)], dst_ref=buffer.at[pl.ds(0, units)], send_sem=send_sem.at[0],
            recv_sem=semaphore, device_id={"pz": q}, device_id_type=MESH,
        ).wait_recv()

    def left(buffer, units, semaphore):
        pltpu.make_async_remote_copy(
            src_ref=buffer.at[pl.ds(0, units)], dst_ref=buffer.at[pl.ds(0, units)], send_sem=semaphore,
            recv_sem=r1.at[0], device_id={"pz": q}, device_id_type=MESH,
        ).wait_send()

    def each_peer(action):
        def step(o, carry):
            action(lax.rem(q + o, NPZ))
            return carry

        lax.fori_loop(1, NPZ, step, 0)

    def start1(c, t, height):
        pltpu.make_async_remote_copy(
            src_ref=zt.at[pl.ds(16 * t + ZC * c, ZC), pl.ds(0, height), :],
            dst_ref=got1.at[pl.ds(ZC * c, ZC), pl.ds(pl.multiple_of(16 * q, 16), height), :],
            send_sem=send_sem.at[0],
            recv_sem=r1.at[c],
            device_id={"pz": t},
            device_id_type=MESH,
        ).start()

    @pl.when(full)
    def _():
        for c in range(CHUNKS):
            each_peer(lambda t: start1(c, t, 16))

    @pl.when(q == 6)
    def _():
        for c in range(CHUNKS):
            each_peer(lambda t: start1(c, t, 8))

    got1[:, pl.ds(pl.multiple_of(16 * q, 16), 16), :] = zt[pl.ds(16 * q, 16), :, :]

    def by_place(when_full, when_half, when_empty):
        pl.when(full)(when_full)
        pl.when(q == 6)(when_half)
        pl.when(jnp.logical_and(q > 6, q < 10))(when_empty)

    def wait1(c):
        by_place(
            lambda: arrived(zt, 11 * ZC + ZC // 2, r1.at[c]),
            lambda: arrived(zt, 12 * ZC, r1.at[c]),
            lambda: arrived(zt, 12 * ZC + ZC // 2, r1.at[c]),
        )

    def rows_pass(c, src, dst):
        z = ZC * c
        done = mm3(table(), split(jnp.concatenate([src[z], src[z + 1]], axis=1)))
        dst[z] = done[:, :128]
        dst[z + 1] = done[:, 128:]

    def start2(c, t):
        pltpu.make_async_remote_copy(
            src_ref=yt.at[pl.ds(ZC * c, ZC), pl.ds(pl.multiple_of(64 * t, 64), 64), :],
            dst_ref=got2.at[p, pl.ds(ZC * c, ZC), :, :],
            send_sem=send_sem.at[1],
            recv_sem=r2.at[c],
            device_id={"py": t},
            device_id_type=MESH,
        ).start()

    def rows_step(c):
        wait1(c)
        rows_pass(c, got1, yt)
        for o in (2, 1, 3):
            start2(c, lax.rem(p + o, NPY))
        got2[p, ZC * c : ZC * c + ZC] = yt[ZC * c : ZC * c + ZC, pl.ds(pl.multiple_of(64 * p, 64), 64), :]

    def wait_py(c, semaphore):
        pltpu.make_async_remote_copy(
            src_ref=got2.at[pl.ds(0, 3), pl.ds(0, ZC)], dst_ref=got2.at[pl.ds(0, 3), pl.ds(0, ZC)],
            send_sem=send_sem.at[1], recv_sem=semaphore, device_id={"py": p}, device_id_type=MESH,
        ).wait_recv()

    lower = iota((ROWS, 128), 1) < 64

    def swap(values):
        return pltpu.roll(values, 64, 1)

    def width_step(c):
        wait_py(c, r2.at[c])
        part = [got2[k, ZC * c : ZC * c + ZC].reshape(ROWS, 128) for k in range(NPY)]
        turned = [swap(value) for value in part]
        first = [jnp.where(lower, part[k], turned[k + 1]) for k in (0, 2)]
        second = [jnp.where(lower, turned[k], part[k + 1]) for k in (0, 2)]
        lines = jnp.concatenate([jnp.concatenate(first, axis=1), jnp.concatenate(second, axis=1)], axis=0)
        real = mm3(split(lines), table())
        field[ROWS * c : ROWS * c + ROWS, :GRID] = real[:ROWS]
        field[ROWS * c : ROWS * c + ROWS, GRID:] = real[ROWS:]

    def gather(c0, c1):
        high, low = split(field[ROWS * c0 : ROWS * c1, :])
        hot = cols_hot[:, ROWS * c0 : ROWS * c1]
        part = mm(hot, high) + mm(hot, low)
        if c0 == 0:
            gathered[...] = part
        else:
            gathered[...] += part

    def one_hot_tables():
        block_row = block[...]
        row_of = lax.shift_right_logical(block_row, 1)
        for k in range(8):
            hot = iota((128, ENT), 0) + 128 * k == jnp.broadcast_to(row_of, (128, ENT))
            rows_hot[128 * k : 128 * k + 128, :] = jnp.where(hot, 1.0, 0.0).astype(BF16)

        eye = iota((ENT, ENT), 0) == iota((ENT, ENT), 1)

        def to_column(row):
            diag = jnp.where(eye, jnp.broadcast_to(row.astype(F32), (ENT, ENT)), 0.0)
            return mm(diag.astype(BF16), jnp.ones((ENT, 128), BF16))

        row_col = 32.0 * to_column(lax.shift_right_logical(row_of, 5)) + to_column(row_of & 31)
        for k in range(8):
            hot = (iota((ENT, 128), 1) + 128 * k).astype(F32) == row_col
            cols_hot[:, 128 * k : 128 * k + 128] = jnp.where(hot, 1.0, 0.0).astype(BF16)
        parity[...] = to_column(block_row & 1)

        atoms = atom[...]
        owner = lax.shift_right_logical(atoms, 6)
        dp = (lax.shift_right_logical(owner, 4) - p) & 3
        dq = ((owner & 15) - q) & 15
        slot = jnp.where(dp == 3, 1, jnp.where(dp == 1, 2, jnp.where(dq == 15, 3, jnp.where(dq == 1, 4, 0))))
        code = slot * 64 + (atoms & 63)
        hot = iota((320, ENT), 0) == jnp.broadcast_to(code, (320, ENT))
        atom_hot[...] = jnp.where(hot, 1.0, 0.0).astype(BF16)

    proj_rows = proj.reshape(ENT * 8, 128)
    lane = iota((ENT, 128), 1)

    def neighbour(s):
        if s < 3:
            return {"py": lax.rem(p + (3 if s == 1 else 1), NPY)}
        return {"pz": lax.rem(q + (15 if s == 3 else 1), NPZ)}

    def copy_terms(rnd, s):
        return pltpu.make_async_remote_copy(
            src_ref=terms.at[rnd, s], dst_ref=terms_in.at[rnd, OPPOSITE[s]], send_sem=st.at[rnd, s],
            recv_sem=rt.at[rnd, OPPOSITE[s]], device_id=neighbour(s), device_id_type=MESH,
        )

    def copy_coupled(rnd, s):
        return pltpu.make_async_remote_copy(
            src_ref=coupled.at[rnd, 0], dst_ref=coupled.at[rnd, OPPOSITE[s]], send_sem=sc.at[rnd, s],
            recv_sem=rc.at[rnd, OPPOSITE[s]], device_id=neighbour(s), device_id_type=MESH,
        )

    def send_terms(rnd):
        odd = parity[...] > 0.5
        entry_terms = jnp.zeros((ENT, 128), F32)
        if rnd == 0:
            whole = gathered[...]
        else:
            high, low = split(field[ROWS * 5 :, :])
            hot = cols_hot[:, ROWS * 5 :]
            whole = gathered[...] + (mm(hot, high) + mm(hot, low))
        for n in range(2):
            cells = jnp.where(odd, whole[:, 256 * n + 128 : 256 * n + 256], whole[:, 256 * n : 256 * n + 128])
            for i in range(8):
                high, low = split(proj_rows[pl.ds(i, ENT, stride=8), :] * cells)
                sums = mm(jnp.concatenate([high, low], axis=1), jnp.ones((256, 128), BF16))
                entry_terms = jnp.where(lane == 8 * n + i, sums, entry_terms)
        high, low = split(entry_terms)
        hot = atom_hot[...]
        terms[rnd] = (mm(hot, high) + mm(hot, low)).reshape(5, 64, 128)
        for s in range(1, 5):
            copy_terms(rnd, s).start()

    def send_coupled(rnd):
        symmetric = 0.5 * (coupling[...] + coupling[...].T)
        place = jnp.where((iota((128, 8), 0) & 7) == iota((128, 8), 1), 1.0, 0.0)
        tiled = jnp.dot(jnp.dot(place, symmetric, precision=HIGHEST), place.T, precision=HIGHEST)
        same = lax.shift_right_logical(iota((128, 128), 0), 3) == lax.shift_right_logical(iota((128, 128), 1), 3)
        mix = jnp.where(same, tiled, 0.0)
        total = terms[rnd, 0]
        for s in range(1, 5):
            copy_terms(rnd, OPPOSITE[s]).wait_recv()
            total = total + terms_in[rnd, s]
        coupled[rnd, 0] = jnp.dot(total, mix, precision=HIGHEST)
        for s in range(1, 5):
            copy_coupled(rnd, s).start()

    def spread_coupled(rnd):
        for s in range(1, 5):
            copy_coupled(rnd, OPPOSITE[s]).wait_recv()
        odd = parity[...]
        hot = atom_hot[...]
        high, low = split(coupled[rnd].reshape(320, 128))
        chosen = mm(hot, high, TN) + mm(hot, low, TN)
        for n in range(2):
            cells = jnp.zeros((ENT, 128), F32)
            for i in range(8):
                j = 8 * n + i
                weight = jnp.broadcast_to(chosen[:, j : j + 1], (ENT, 128))
                cells += proj_rows[pl.ds(i, ENT, stride=8), :] * weight
            for half in range(2):
                high, low = split(jnp.where(odd > 0.5, cells if half else 0.0, 0.0 if half else cells))
                lanes = slice(256 * n + 128 * half, 256 * n + 128 * half + 128)
                spread_hi[:, lanes] = high
                spread_lo[:, lanes] = low

    def start3(c, t):
        pltpu.make_async_remote_copy(
            src_ref=xb.at[t, pl.ds(ZC * c, ZC), :, :],
            dst_ref=got3.at[pl.ds(ZC * c, ZC), pl.ds(pl.multiple_of(64 * p, 64), 64), :],
            send_sem=send_sem.at[2],
            recv_sem=r3.at[c],
            device_id={"py": t},
            device_id_type=MESH,
        ).start()

    def back_step(c0, c1):
        rows = slice(ROWS * c0, ROWS * c1)
        hot = rows_hot[rows, :]
        placed = mm(hot, spread_hi[...]) + mm(hot, spread_lo[...])
        count = ROWS * (c1 - c0)
        local = pot[ZC * c0 : ZC * c1].reshape(count, GRID)
        whole = [local * field[rows, GRID * n : GRID * n + GRID] + placed[:, GRID * n : GRID * n + GRID] for n in range(2)]
        done = mm3(split(jnp.concatenate(whole, axis=0)), table())
        for c in range(c0, c1):
            top = ROWS * (c - c0)
            for h in range(2):
                first = done[top : top + ROWS, 128 * h : 128 * h + 128]
                second = done[count + top : count + top + ROWS, 128 * h : 128 * h + 128]
                xb[2 * h, ZC * c : ZC * c + ZC] = jnp.where(lower, first, swap(second)).reshape(ZC, 64, 128)
                xb[2 * h + 1, ZC * c : ZC * c + ZC] = jnp.where(lower, swap(first), second).reshape(ZC, 64, 128)
            for o in (2, 1, 3):
                start3(c, lax.rem(p + o, NPY))
            got3[ZC * c : ZC * c + ZC, pl.ds(pl.multiple_of(64 * p, 64), 64), :] = xb[p, ZC * c : ZC * c + ZC]

    def start4(c, t, height):
        pltpu.make_async_remote_copy(
            src_ref=yb.at[pl.ds(ZC * c, ZC), pl.ds(pl.multiple_of(16 * t, 16), height), :],
            dst_ref=got4.at[pl.ds(16 * q + ZC * c, ZC), pl.ds(0, height), :],
            send_sem=send_sem.at[3],
            recv_sem=r4,
            device_id={"pz": t},
            device_id_type=MESH,
        ).start()

    def final_rows(c):
        wait_py(c, r3.at[c])
        rows_pass(c, got3, yb)

        def one(t):
            @pl.when(jnp.logical_or(t < 6, t > 9))
            def _():
                start4(c, t, 16)

            @pl.when(t == 6)
            def _():
                start4(c, t, 8)

        each_peer(one)

    apart(one_hot_tables)
    for c in range(CHUNKS):
        apart(functools.partial(rows_step, c))
    for load in loads:
        load.wait()
    apart(functools.partial(width_step, 0))
    apart(functools.partial(width_step, 1))
    apart(functools.partial(gather, 0, 2))
    apart(functools.partial(width_step, 2))
    apart(functools.partial(width_step, 3))
    apart(functools.partial(gather, 2, 4))
    apart(functools.partial(width_step, 4))
    apart(functools.partial(gather, 4, 5))
    apart(functools.partial(send_terms, 0))
    apart(functools.partial(width_step, 5))
    apart(functools.partial(send_coupled, 0))
    apart(functools.partial(width_step, 6))
    apart(functools.partial(spread_coupled, 0))
    apart(functools.partial(back_step, 1, 2))
    apart(functools.partial(back_step, 2, 4))
    apart(functools.partial(width_step, 7))
    apart(functools.partial(send_terms, 1))
    apart(functools.partial(final_rows, 1))
    apart(functools.partial(send_coupled, 1))
    apart(functools.partial(final_rows, 2))
    apart(functools.partial(spread_coupled, 1))
    apart(functools.partial(back_step, 4, 6))
    apart(functools.partial(back_step, 6, 8))
    apart(functools.partial(back_step, 0, 1))
    for c in (3, 4, 5, 6, 7, 0):
        apart(functools.partial(final_rows, c))
    got4[pl.ds(16 * q, 16), :, :] = yb[:, pl.ds(pl.multiple_of(16 * q, 16), 16), :]

    pl.when(full)(lambda: left(zt, 15 * 16, send_sem.at[0]))
    pl.when(q == 6)(lambda: left(zt, 15 * 8, send_sem.at[0]))
    for k in (1, 2):
        pltpu.make_async_remote_copy(
            src_ref=got2.at[pl.ds(0, 3)], dst_ref=got2.at[pl.ds(0, 3)], send_sem=send_sem.at[k], recv_sem=r2.at[0],
            device_id={"py": p}, device_id_type=MESH,
        ).wait_send()
    for rnd in range(2):
        for s in range(1, 5):
            copy_terms(rnd, s).wait_send()
            copy_coupled(rnd, s).wait_send()

    pl.when(full)(lambda: arrived(zt, 15 * 16, r4))
    pl.when(q == 6)(lambda: arrived(zt, 15 * 8, r4))

    got4_rows = got4.reshape(4096, 128)

    def final_step(y, carry):
        keep = inside(y)
        lines = got4_rows[pl.ds(y, GRID, stride=16), :]
        done = mm3(split(lines), table(), TN)
        fy = freq(16 * q + y)
        fx = freq(64 * p + iota((64, GRID), 0))
        fz = freq(iota((64, GRID), 1))
        kinetic = (fz * fz + fx * fx + fy * fy).astype(F32) * (0.5 * (4.0 / GRID) ** 2)
        for n in range(2):
            result[n, y] = jnp.where(keep, kinetic * coef[n, y] + done[64 * n : 64 * n + 64, :], 0.0)
        return carry

    writes = []
    for k in range(4):
        lax.fori_loop(4 * k, 4 * k + 4, final_step, 0, unroll=4)
        writes.append(
            pltpu.make_async_copy(result.at[:, 4 * k : 4 * k + 4], out_any.at[:, 4 * k : 4 * k + 4], out_sem.at[k])
        )
        writes[-1].start()
    by_place(
        lambda: left(zt, 11 * 16 + 8, send_sem.at[3]),
        lambda: left(zt, 12 * 16, send_sem.at[3]),
        lambda: left(zt, 12 * 16 + 8, send_sem.at[3]),
    )
    for write in writes:
        write.wait()


def shards(coefficients, potential, column_limit, entry_atom, entry_block, projectors, coupling):
    vmem = pl.BlockSpec(memory_space=pltpu.VMEM)
    anywhere = pl.BlockSpec(memory_space=pl.ANY)
    big = pltpu.VMEM((16, 256, 128), F32)
    dma = pltpu.SemaphoreType.DMA
    return pl.pallas_call(
        kernel,
        name="hamiltonian",
        out_shape=jax.ShapeDtypeStruct(coefficients.shape, F32),
        in_specs=[vmem] * 6 + [anywhere] * 3,
        out_specs=anywhere,
        scratch_shapes=[
            pltpu.VMEM((2, 16, 64, GRID), F32),
            pltpu.VMEM((16, 64, GRID), F32),
            pltpu.VMEM((ENT, 8, 128), F32),
            pltpu.VMEM((2, 16, 64, GRID), F32),
            pltpu.VMEM((256, 16, 128), F32),
            big,
            big,
            pltpu.VMEM((NPY, 16, 64, 128), F32),
            pltpu.VMEM((1024, 512), F32),
            pltpu.VMEM((NPY, 16, 64, 128), F32),
            big,
            big,
            pltpu.VMEM((256, 16, 128), F32),
            pltpu.VMEM((1024, ENT), BF16),
            pltpu.VMEM((ENT, 1024), BF16),
            pltpu.VMEM((ENT, 128), F32),
            pltpu.VMEM((320, ENT), BF16),
            pltpu.VMEM((ENT, 512), F32),
            pltpu.VMEM((ENT, 512), BF16),
            pltpu.VMEM((ENT, 512), BF16),
            pltpu.VMEM((2, 5, 64, 128), F32),
            pltpu.VMEM((2, 5, 64, 128), F32),
            pltpu.VMEM((2, 5, 64, 128), F32),
            dma((2,)),
            dma((4,)),
            dma((4,)),
            dma((4,)),
            dma((CHUNKS,)),
            dma((CHUNKS,)),
            dma((CHUNKS,)),
            dma,
            dma((2, 5)),
            dma((2, 5)),
            dma((2, 5)),
            dma((2, 5)),
        ],
        compiler_params=pltpu.CompilerParams(
            collective_id=0, has_side_effects=True, vmem_limit_bytes=56 * 2**20
        ),
    )(
        column_limit,
        entry_atom.reshape(1, ENT),
        entry_block.reshape(1, ENT),
        coupling,
        *(jnp.asarray(table) for table in halves(cas_matrix())),
        coefficients,
        potential,
        projectors,
    )


def solution(mesh):
    in_specs = (
        P("band", "pz", "py", None),
        P("pz", "py", None),
        P("pz", "py"),
        P(("py", "pz"), None),
        P(("py", "pz")),
        P(("py", "pz"), None, None),
        P(),
    )
    out_specs = P("band", "pz", "py", None)
    return jax.shard_map(shards, mesh=mesh, in_specs=in_specs, out_specs=out_specs, check_vma=False)
```

```python
import functools
import math

import jax
import jax.numpy as jnp
import numpy as np
from jax import lax
from jax.experimental import pallas as pl
from jax.experimental.pallas import tpu as pltpu
from jax.sharding import PartitionSpec as P

F32 = jnp.float32
BF16 = jnp.bfloat16
I32 = jnp.int32
MESH = pl.DeviceIdType.MESH
HIGHEST = lax.Precision.HIGHEST

NPY, NPZ = 4, 16
GRID = 256
CHUNKS = 8
ZC = 2
ROWS = 64 * ZC
ENT = 512
OPPOSITE = (0, 2, 1, 4, 3)


def cas_matrix():
    index = np.arange(GRID)
    angle = (index[:, None] * index[None, :] % GRID) * (2.0 * math.pi / GRID)
    return ((np.cos(angle) + np.sin(angle)) / math.sqrt(GRID)).astype(np.float32)


def halves(table):
    high = table.astype(jnp.bfloat16)
    low = (table - high.astype(np.float32)).astype(jnp.bfloat16)
    return high, low


def split(values):
    high = values.astype(BF16)
    return high, (values - high.astype(F32)).astype(BF16)


NN = (((1,), (0,)), ((), ()))
NT = (((1,), (1,)), ((), ()))
TN = (((0,), (0,)), ((), ()))


def mm(a, b, dims=NN):
    return lax.dot_general(a, b, dims, preferred_element_type=F32)


def mm3(a, b, dims=NN):
    (a_high, a_low), (b_high, b_low) = a, b
    return mm(a_high, b_high, dims) + (mm(a_high, b_low, dims) + mm(a_low, b_high, dims))


def iota(shape, dim):
    return lax.broadcasted_iota(I32, shape, dim)


def freq(index):
    return jnp.minimum(index, GRID - index)


def kernel(
    limit, atom, block, coupling, chi, clo, coef_any, pot_any, proj_any,
    out_any,
    coef, pot, proj, result,
    zt, got1, yt, got2, field, xb, got3, yb, got4,
    rows_hot, cols_hot, parity, atom_hot, gathered, spread_hi, spread_lo, terms, terms_in, coupled,
    local_sem, coef_sem, out_sem, send_sem, r1, r2, r3, r4, st, rt, sc, rc,
):
    p = lax.axis_index("py")
    q = lax.axis_index("pz")
    full = jnp.logical_or(q < 6, q > 9)

    coef_loads = [
        pltpu.make_async_copy(coef_any.at[:, 4 * k : 4 * k + 4], coef.at[:, 4 * k : 4 * k + 4], coef_sem.at[k])
        for k in range(4)
    ]
    loads = [
        pltpu.make_async_copy(proj_any, proj, local_sem.at[0]),
        pltpu.make_async_copy(pot_any, pot, local_sem.at[1]),
    ]
    for load in coef_loads + loads:
        load.start()

    got1[:, 96:160, :] = jnp.zeros((16, 64, 128), F32)

    barrier = pltpu.get_barrier_semaphore()
    for o in range(1, NPZ):
        pl.semaphore_signal(barrier, inc=1, device_id={"pz": lax.rem(q + o, NPZ)}, device_id_type=MESH)
    for o in range(1, NPY):
        pl.semaphore_signal(barrier, inc=1, device_id={"py": lax.rem(p + o, NPY)}, device_id_type=MESH)

    def table():
        return chi[...], clo[...]

    def apart(work):
        pl.when(q >= 0)(work)

    def inside(y):
        row = limit[pl.ds(y, 1), :].astype(F32)
        diag = jnp.where(iota((64, 64), 0) == iota((64, 64), 1), jnp.broadcast_to(row, (64, 64)), 0.0)
        bound = mm(diag.astype(BF16), jnp.ones((64, GRID), BF16))
        return freq(iota((64, GRID), 1)).astype(F32) <= bound

    zt_rows = zt.reshape(4096, 128)

    def depth_step(y, carry):
        keep = inside(y)
        pair = jnp.concatenate([jnp.where(keep, coef[0, y], 0.0), jnp.where(keep, coef[1, y], 0.0)], axis=0)
        zt_rows[pl.ds(y, GRID, stride=16), :] = mm3(table(), split(pair), NT)
        return carry

    for k in range(4):
        coef_loads[k].wait()
        lax.fori_loop(4 * k, 4 * k + 4, depth_step, 0, unroll=4)

    pl.semaphore_wait(barrier, NPZ + NPY - 2)

    def arrived(buffer, units, semaphore):
        pltpu.make_async_remote_copy(
            src_ref=buffer.at[pl.ds(0, units)], dst_ref=buffer.at[pl.ds(0, units)], send_sem=send_sem.at[0],
            recv_sem=semaphore, device_id={"pz": q}, device_id_type=MESH,
        ).wait_recv()

    def left(buffer, units, semaphore):
        pltpu.make_async_remote_copy(
            src_ref=buffer.at[pl.ds(0, units)], dst_ref=buffer.at[pl.ds(0, units)], send_sem=semaphore,
            recv_sem=r1.at[0], device_id={"pz": q}, device_id_type=MESH,
        ).wait_send()

    def each_peer(action):
        def step(o, carry):
            action(lax.rem(q + o, NPZ))
            return carry

        lax.fori_loop(1, NPZ, step, 0)

    def start1(c, t, height):
        pltpu.make_async_remote_copy(
            src_ref=zt.at[pl.ds(16 * t + ZC * c, ZC), pl.ds(0, height), :],
            dst_ref=got1.at[pl.ds(ZC * c, ZC), pl.ds(pl.multiple_of(16 * q, 16), height), :],
            send_sem=send_sem.at[0],
            recv_sem=r1.at[c],
            device_id={"pz": t},
            device_id_type=MESH,
        ).start()

    @pl.when(full)
    def _():
        for c in range(CHUNKS):
            each_peer(lambda t: start1(c, t, 16))

    @pl.when(q == 6)
    def _():
        for c in range(CHUNKS):
            each_peer(lambda t: start1(c, t, 8))

    got1[:, pl.ds(pl.multiple_of(16 * q, 16), 16), :] = zt[pl.ds(16 * q, 16), :, :]

    def by_place(when_full, when_half, when_empty):
        pl.when(full)(when_full)
        pl.when(q == 6)(when_half)
        pl.when(jnp.logical_and(q > 6, q < 10))(when_empty)

    def wait1(c):
        by_place(
            lambda: arrived(zt, 11 * ZC + ZC // 2, r1.at[c]),
            lambda: arrived(zt, 12 * ZC, r1.at[c]),
            lambda: arrived(zt, 12 * ZC + ZC // 2, r1.at[c]),
        )

    def rows_pass(c, src, dst):
        z = ZC * c
        done = mm3(table(), split(jnp.concatenate([src[z], src[z + 1]], axis=1)))
        dst[z] = done[:, :128]
        dst[z + 1] = done[:, 128:]

    def start2(c, t):
        pltpu.make_async_remote_copy(
            src_ref=yt.at[pl.ds(ZC * c, ZC), pl.ds(pl.multiple_of(64 * t, 64), 64), :],
            dst_ref=got2.at[p, pl.ds(ZC * c, ZC), :, :],
            send_sem=send_sem.at[1],
            recv_sem=r2.at[c],
            device_id={"py": t},
            device_id_type=MESH,
        ).start()

    def send2(c):
        for o in (1, 3, 2):
            start2(c, lax.rem(p + o, NPY))

    def rows_step(c):
        wait1(c)
        rows_pass(c, got1, yt)
        got2[p, ZC * c : ZC * c + ZC] = yt[ZC * c : ZC * c + ZC, pl.ds(pl.multiple_of(64 * p, 64), 64), :]

    def wait_py(c, semaphore):
        pltpu.make_async_remote_copy(
            src_ref=got2.at[pl.ds(0, 3), pl.ds(0, ZC)], dst_ref=got2.at[pl.ds(0, 3), pl.ds(0, ZC)],
            send_sem=send_sem.at[1], recv_sem=semaphore, device_id={"py": p}, device_id_type=MESH,
        ).wait_recv()

    lower = iota((ROWS, 128), 1) < 64

    def swap(values):
        return pltpu.roll(values, 64, 1)

    def width_step(c):
        wait_py(c, r2.at[c])
        part = [got2[k, ZC * c : ZC * c + ZC].reshape(ROWS, 128) for k in range(NPY)]
        turned = [swap(value) for value in part]
        first = [jnp.where(lower, part[k], turned[k + 1]) for k in (0, 2)]
        second = [jnp.where(lower, turned[k], part[k + 1]) for k in (0, 2)]
        lines = jnp.concatenate([jnp.concatenate(first, axis=1), jnp.concatenate(second, axis=1)], axis=0)
        real = mm3(split(lines), table())
        field[ROWS * c : ROWS * c + ROWS, :GRID] = real[:ROWS]
        field[ROWS * c : ROWS * c + ROWS, GRID:] = real[ROWS:]

    def gather(c0, c1):
        high, low = split(field[ROWS * c0 : ROWS * c1, :])
        hot = cols_hot[:, ROWS * c0 : ROWS * c1]
        part = mm(hot, high) + mm(hot, low)
        if c0 == 0:
            gathered[...] = part
        else:
            gathered[...] += part

    def one_hot_tables():
        block_row = block[...]
        row_of = lax.shift_right_logical(block_row, 1)
        for k in range(8):
            hot = iota((128, ENT), 0) + 128 * k == jnp.broadcast_to(row_of, (128, ENT))
            rows_hot[128 * k : 128 * k + 128, :] = jnp.where(hot, 1.0, 0.0).astype(BF16)

        eye = iota((ENT, ENT), 0) == iota((ENT, ENT), 1)

        def to_column(row):
            diag = jnp.where(eye, jnp.broadcast_to(row.astype(F32), (ENT, ENT)), 0.0)
            return mm(diag.astype(BF16), jnp.ones((ENT, 128), BF16))

        row_col = 32.0 * to_column(lax.shift_right_logical(row_of, 5)) + to_column(row_of & 31)
        for k in range(8):
            hot = (iota((ENT, 128), 1) + 128 * k).astype(F32) == row_col
            cols_hot[:, 128 * k : 128 * k + 128] = jnp.where(hot, 1.0, 0.0).astype(BF16)
        parity[...] = to_column(block_row & 1)

        atoms = atom[...]
        owner = lax.shift_right_logical(atoms, 6)
        dp = (lax.shift_right_logical(owner, 4) - p) & 3
        dq = ((owner & 15) - q) & 15
        slot = jnp.where(dp == 3, 1, jnp.where(dp == 1, 2, jnp.where(dq == 15, 3, jnp.where(dq == 1, 4, 0))))
        code = slot * 64 + (atoms & 63)
        hot = iota((320, ENT), 0) == jnp.broadcast_to(code, (320, ENT))
        atom_hot[...] = jnp.where(hot, 1.0, 0.0).astype(BF16)

    proj_rows = proj.reshape(ENT * 8, 128)
    lane = iota((ENT, 128), 1)

    def neighbour(s):
        if s < 3:
            return {"py": lax.rem(p + (3 if s == 1 else 1), NPY)}
        return {"pz": lax.rem(q + (15 if s == 3 else 1), NPZ)}

    def copy_terms(rnd, s):
        return pltpu.make_async_remote_copy(
            src_ref=terms.at[rnd, s], dst_ref=terms_in.at[rnd, OPPOSITE[s]], send_sem=st.at[rnd, s],
            recv_sem=rt.at[rnd, OPPOSITE[s]], device_id=neighbour(s), device_id_type=MESH,
        )

    def copy_coupled(rnd, s):
        return pltpu.make_async_remote_copy(
            src_ref=coupled.at[rnd, 0], dst_ref=coupled.at[rnd, OPPOSITE[s]], send_sem=sc.at[rnd, s],
            recv_sem=rc.at[rnd, OPPOSITE[s]], device_id=neighbour(s), device_id_type=MESH,
        )

    def send_terms(rnd):
        odd = parity[...] > 0.5
        entry_terms = jnp.zeros((ENT, 128), F32)
        if rnd == 0:
            whole = gathered[...]
        else:
            high, low = split(field[ROWS * 5 :, :])
            hot = cols_hot[:, ROWS * 5 :]
            whole = gathered[...] + (mm(hot, high) + mm(hot, low))
        for n in range(2):
            cells = jnp.where(odd, whole[:, 256 * n + 128 : 256 * n + 256], whole[:, 256 * n : 256 * n + 128])
            for i in range(8):
                high, low = split(proj_rows[pl.ds(i, ENT, stride=8), :] * cells)
                sums = mm(jnp.concatenate([high, low], axis=1), jnp.ones((256, 128), BF16))
                entry_terms = jnp.where(lane == 8 * n + i, sums, entry_terms)
        high, low = split(entry_terms)
        hot = atom_hot[...]
        terms[rnd] = (mm(hot, high) + mm(hot, low)).reshape(5, 64, 128)
        for s in range(1, 5):
            copy_terms(rnd, s).start()

    def send_coupled(rnd):
        symmetric = 0.5 * (coupling[...] + coupling[...].T)
        place = jnp.where((iota((128, 8), 0) & 7) == iota((128, 8), 1), 1.0, 0.0)
        tiled = jnp.dot(jnp.dot(place, symmetric, precision=HIGHEST), place.T, precision=HIGHEST)
        same = lax.shift_right_logical(iota((128, 128), 0), 3) == lax.shift_right_logical(iota((128, 128), 1), 3)
        mix = jnp.where(same, tiled, 0.0)
        total = terms[rnd, 0]
        for s in range(1, 5):
            copy_terms(rnd, OPPOSITE[s]).wait_recv()
            total = total + terms_in[rnd, s]
        coupled[rnd, 0] = jnp.dot(total, mix, precision=HIGHEST)
        for s in range(1, 5):
            copy_coupled(rnd, s).start()

    def spread_coupled(rnd):
        for s in range(1, 5):
            copy_coupled(rnd, OPPOSITE[s]).wait_recv()
        odd = parity[...]
        hot = atom_hot[...]
        high, low = split(coupled[rnd].reshape(320, 128))
        chosen = mm(hot, high, TN) + mm(hot, low, TN)
        for n in range(2):
            cells = jnp.zeros((ENT, 128), F32)
            for i in range(8):
                j = 8 * n + i
                weight = jnp.broadcast_to(chosen[:, j : j + 1], (ENT, 128))
                cells += proj_rows[pl.ds(i, ENT, stride=8), :] * weight
            for half in range(2):
                high, low = split(jnp.where(odd > 0.5, cells if half else 0.0, 0.0 if half else cells))
                lanes = slice(256 * n + 128 * half, 256 * n + 128 * half + 128)
                spread_hi[:, lanes] = high
                spread_lo[:, lanes] = low

    def start3(c, t):
        pltpu.make_async_remote_copy(
            src_ref=xb.at[t, pl.ds(ZC * c, ZC), :, :],
            dst_ref=got3.at[pl.ds(ZC * c, ZC), pl.ds(pl.multiple_of(64 * p, 64), 64), :],
            send_sem=send_sem.at[2],
            recv_sem=r3.at[c],
            device_id={"py": t},
            device_id_type=MESH,
        ).start()

    def send3(c):
        for o in (1, 3, 2):
            start3(c, lax.rem(p + o, NPY))

    def back_step(c0, c1):
        rows = slice(ROWS * c0, ROWS * c1)
        hot = rows_hot[rows, :]
        placed = mm(hot, spread_hi[...]) + mm(hot, spread_lo[...])
        count = ROWS * (c1 - c0)
        local = pot[ZC * c0 : ZC * c1].reshape(count, GRID)
        whole = [local * field[rows, GRID * n : GRID * n + GRID] + placed[:, GRID * n : GRID * n + GRID] for n in range(2)]
        done = mm3(split(jnp.concatenate(whole, axis=0)), table())
        for c in range(c0, c1):
            top = ROWS * (c - c0)
            for h in range(2):
                first = done[top : top + ROWS, 128 * h : 128 * h + 128]
                second = done[count + top : count + top + ROWS, 128 * h : 128 * h + 128]
                xb[2 * h, ZC * c : ZC * c + ZC] = jnp.where(lower, first, swap(second)).reshape(ZC, 64, 128)
                xb[2 * h + 1, ZC * c : ZC * c + ZC] = jnp.where(lower, swap(first), second).reshape(ZC, 64, 128)
            got3[ZC * c : ZC * c + ZC, pl.ds(pl.multiple_of(64 * p, 64), 64), :] = xb[p, ZC * c : ZC * c + ZC]

    def start4(c, t, height):
        pltpu.make_async_remote_copy(
            src_ref=yb.at[pl.ds(ZC * c, ZC), pl.ds(pl.multiple_of(16 * t, 16), height), :],
            dst_ref=got4.at[pl.ds(16 * q + ZC * c, ZC), pl.ds(0, height), :],
            send_sem=send_sem.at[3],
            recv_sem=r4,
            device_id={"pz": t},
            device_id_type=MESH,
        ).start()

    def final_rows(c):
        wait_py(c, r3.at[c])
        rows_pass(c, got3, yb)

    def send4(c):
        def one(t):
            @pl.when(jnp.logical_or(t < 6, t > 9))
            def _():
                start4(c, t, 16)

            @pl.when(t == 6)
            def _():
                start4(c, t, 8)

        each_peer(one)

    apart(one_hot_tables)
    for c in range(CHUNKS):
        apart(functools.partial(rows_step, c))
        if c < 2:
            send2(c)
    for load in loads:
        load.wait()
    apart(functools.partial(width_step, 0))
    send2(2)
    apart(functools.partial(width_step, 1))
    send2(3)
    apart(functools.partial(gather, 0, 2))
    apart(functools.partial(width_step, 2))
    send2(4)
    apart(functools.partial(width_step, 3))
    send2(5)
    apart(functools.partial(gather, 2, 4))
    apart(functools.partial(width_step, 4))
    apart(functools.partial(gather, 4, 5))
    apart(functools.partial(send_terms, 0))
    send2(6)
    apart(functools.partial(width_step, 5))
    apart(functools.partial(send_coupled, 0))
    send2(7)
    apart(functools.partial(width_step, 6))
    apart(functools.partial(spread_coupled, 0))
    apart(functools.partial(back_step, 1, 2))
    send3(1)
    apart(functools.partial(width_step, 7))
    apart(functools.partial(send_terms, 1))
    apart(functools.partial(back_step, 2, 4))
    send3(2)
    apart(functools.partial(final_rows, 1))
    apart(functools.partial(send_coupled, 1))
    send3(3)
    send4(1)
    apart(functools.partial(final_rows, 2))
    apart(functools.partial(spread_coupled, 1))
    apart(functools.partial(back_step, 4, 6))
    send3(4)
    send3(5)
    send4(2)
    apart(functools.partial(back_step, 6, 8))
    send3(6)
    send3(7)
    apart(functools.partial(back_step, 0, 1))
    send3(0)
    for c in (3, 4, 5, 6, 7, 0):
        apart(functools.partial(final_rows, c))
        send4(c)
    got4[pl.ds(16 * q, 16), :, :] = yb[:, pl.ds(pl.multiple_of(16 * q, 16), 16), :]

    pl.when(full)(lambda: left(zt, 15 * 16, send_sem.at[0]))
    pl.when(q == 6)(lambda: left(zt, 15 * 8, send_sem.at[0]))
    for k in (1, 2):
        pltpu.make_async_remote_copy(
            src_ref=got2.at[pl.ds(0, 3)], dst_ref=got2.at[pl.ds(0, 3)], send_sem=send_sem.at[k], recv_sem=r2.at[0],
            device_id={"py": p}, device_id_type=MESH,
        ).wait_send()
    for rnd in range(2):
        for s in range(1, 5):
            copy_terms(rnd, s).wait_send()
            copy_coupled(rnd, s).wait_send()

    pl.when(full)(lambda: arrived(zt, 15 * 16, r4))
    pl.when(q == 6)(lambda: arrived(zt, 15 * 8, r4))

    got4_rows = got4.reshape(4096, 128)

    def final_step(y, carry):
        keep = inside(y)
        lines = got4_rows[pl.ds(y, GRID, stride=16), :]
        done = mm3(split(lines), table(), TN)
        fy = freq(16 * q + y)
        fx = freq(64 * p + iota((64, GRID), 0))
        fz = freq(iota((64, GRID), 1))
        kinetic = (fz * fz + fx * fx + fy * fy).astype(F32) * (0.5 * (4.0 / GRID) ** 2)
        for n in range(2):
            result[n, y] = jnp.where(keep, kinetic * coef[n, y] + done[64 * n : 64 * n + 64, :], 0.0)
        return carry

    writes = []
    for k in range(4):
        lax.fori_loop(4 * k, 4 * k + 4, final_step, 0, unroll=4)
        writes.append(
            pltpu.make_async_copy(result.at[:, 4 * k : 4 * k + 4], out_any.at[:, 4 * k : 4 * k + 4], out_sem.at[k])
        )
        writes[-1].start()
    by_place(
        lambda: left(zt, 11 * 16 + 8, send_sem.at[3]),
        lambda: left(zt, 12 * 16, send_sem.at[3]),
        lambda: left(zt, 12 * 16 + 8, send_sem.at[3]),
    )
    for write in writes:
        write.wait()


def shards(coefficients, potential, column_limit, entry_atom, entry_block, projectors, coupling):
    vmem = pl.BlockSpec(memory_space=pltpu.VMEM)
    anywhere = pl.BlockSpec(memory_space=pl.ANY)
    big = pltpu.VMEM((16, 256, 128), F32)
    dma = pltpu.SemaphoreType.DMA
    return pl.pallas_call(
        kernel,
        name="hamiltonian",
        out_shape=jax.ShapeDtypeStruct(coefficients.shape, F32),
        in_specs=[vmem] * 6 + [anywhere] * 3,
        out_specs=anywhere,
        scratch_shapes=[
            pltpu.VMEM((2, 16, 64, GRID), F32),
            pltpu.VMEM((16, 64, GRID), F32),
            pltpu.VMEM((ENT, 8, 128), F32),
            pltpu.VMEM((2, 16, 64, GRID), F32),
            pltpu.VMEM((256, 16, 128), F32),
            big,
            big,
            pltpu.VMEM((NPY, 16, 64, 128), F32),
            pltpu.VMEM((1024, 512), F32),
            pltpu.VMEM((NPY, 16, 64, 128), F32),
            big,
            big,
            pltpu.VMEM((256, 16, 128), F32),
            pltpu.VMEM((1024, ENT), BF16),
            pltpu.VMEM((ENT, 1024), BF16),
            pltpu.VMEM((ENT, 128), F32),
            pltpu.VMEM((320, ENT), BF16),
            pltpu.VMEM((ENT, 512), F32),
            pltpu.VMEM((ENT, 512), BF16),
            pltpu.VMEM((ENT, 512), BF16),
            pltpu.VMEM((2, 5, 64, 128), F32),
            pltpu.VMEM((2, 5, 64, 128), F32),
            pltpu.VMEM((2, 5, 64, 128), F32),
            dma((2,)),
            dma((4,)),
            dma((4,)),
            dma((4,)),
            dma((CHUNKS,)),
            dma((CHUNKS,)),
            dma((CHUNKS,)),
            dma,
            dma((2, 5)),
            dma((2, 5)),
            dma((2, 5)),
            dma((2, 5)),
        ],
        compiler_params=pltpu.CompilerParams(
            collective_id=0, has_side_effects=True, vmem_limit_bytes=56 * 2**20
        ),
    )(
        column_limit,
        entry_atom.reshape(1, ENT),
        entry_block.reshape(1, ENT),
        coupling,
        *(jnp.asarray(table) for table in halves(cas_matrix())),
        coefficients,
        potential,
        projectors,
    )


def solution(mesh):
    in_specs = (
        P("band", "pz", "py", None),
        P("pz", "py", None),
        P("pz", "py"),
        P(("py", "pz"), None),
        P(("py", "pz")),
        P(("py", "pz"), None, None),
        P(),
    )
    out_specs = P("band", "pz", "py", None)
    return jax.shard_map(shards, mesh=mesh, in_specs=in_specs, out_specs=out_specs, check_vma=False)
```

```python
import functools
import math

import jax
import jax.numpy as jnp
import numpy as np
from jax import lax
from jax.experimental import pallas as pl
from jax.experimental.pallas import tpu as pltpu
from jax.sharding import PartitionSpec as P

F32 = jnp.float32
BF16 = jnp.bfloat16
I32 = jnp.int32
MESH = pl.DeviceIdType.MESH
HIGHEST = lax.Precision.HIGHEST

NPY, NPZ = 4, 16
GRID = 256
CHUNKS = 8
ZC = 2
ROWS = 64 * ZC
ENT = 512
OPPOSITE = (0, 2, 1, 4, 3)


def cas_matrix():
    index = np.arange(GRID)
    angle = (index[:, None] * index[None, :] % GRID) * (2.0 * math.pi / GRID)
    return ((np.cos(angle) + np.sin(angle)) / math.sqrt(GRID)).astype(np.float32)


def halves(table):
    high = table.astype(jnp.bfloat16)
    low = (table - high.astype(np.float32)).astype(jnp.bfloat16)
    return high, low


def split(values):
    high = values.astype(BF16)
    return high, (values - high.astype(F32)).astype(BF16)


NN = (((1,), (0,)), ((), ()))
NT = (((1,), (1,)), ((), ()))
TN = (((0,), (0,)), ((), ()))


def mm(a, b, dims=NN):
    return lax.dot_general(a, b, dims, preferred_element_type=F32)


def mm3(a, b, dims=NN):
    (a_high, a_low), (b_high, b_low) = a, b
    return mm(a_high, b_high, dims) + (mm(a_high, b_low, dims) + mm(a_low, b_high, dims))


def iota(shape, dim):
    return lax.broadcasted_iota(I32, shape, dim)


def freq(index):
    return jnp.minimum(index, GRID - index)


def inside(limit, y):
    row = limit[pl.ds(y, 1), :].astype(F32)
    diag = jnp.where(iota((64, 64), 0) == iota((64, 64), 1), jnp.broadcast_to(row, (64, 64)), 0.0)
    bound = mm(diag.astype(BF16), jnp.ones((64, GRID), BF16))
    return freq(iota((64, GRID), 1)).astype(F32) <= bound


def kernel(
    limit, atom, block, coupling, chi, clo, coef_any, pot_any, proj_any,
    got4,
    coef, pot, proj,
    zt, got1, yt, got2, field, xb, got3, yb,
    rows_hot, cols_hot, parity, atom_hot, gathered, spread_hi, spread_lo, terms, terms_in, coupled,
    local_sem, coef_sem, send_sem, r1, r2, r3, r4, st, rt, sc, rc,
):
    p = lax.axis_index("py")
    q = lax.axis_index("pz")
    full = jnp.logical_or(q < 6, q > 9)

    coef_loads = [
        pltpu.make_async_copy(coef_any.at[:, 4 * k : 4 * k + 4], coef.at[:, 4 * k : 4 * k + 4], coef_sem.at[k])
        for k in range(4)
    ]
    loads = [
        pltpu.make_async_copy(proj_any, proj, local_sem.at[0]),
        pltpu.make_async_copy(pot_any, pot, local_sem.at[1]),
    ]
    for load in coef_loads + loads:
        load.start()

    got1[:, 96:160, :] = jnp.zeros((16, 64, 128), F32)

    barrier = pltpu.get_barrier_semaphore()
    for o in range(1, NPZ):
        pl.semaphore_signal(barrier, inc=1, device_id={"pz": lax.rem(q + o, NPZ)}, device_id_type=MESH)
    for o in range(1, NPY):
        pl.semaphore_signal(barrier, inc=1, device_id={"py": lax.rem(p + o, NPY)}, device_id_type=MESH)

    def table():
        return chi[...], clo[...]

    def apart(work):
        pl.when(q >= 0)(work)

    zt_rows = zt.reshape(4096, 128)

    def depth_step(y, carry):
        keep = inside(limit, y)
        pair = jnp.concatenate([jnp.where(keep, coef[0, y], 0.0), jnp.where(keep, coef[1, y], 0.0)], axis=0)
        zt_rows[pl.ds(y, GRID, stride=16), :] = mm3(table(), split(pair), NT)
        return carry

    for k in range(4):
        coef_loads[k].wait()
        lax.fori_loop(4 * k, 4 * k + 4, depth_step, 0, unroll=4)

    pl.semaphore_wait(barrier, NPZ + NPY - 2)

    def arrived(buffer, units, semaphore):
        pltpu.make_async_remote_copy(
            src_ref=buffer.at[pl.ds(0, units)], dst_ref=buffer.at[pl.ds(0, units)], send_sem=send_sem.at[0],
            recv_sem=semaphore, device_id={"pz": q}, device_id_type=MESH,
        ).wait_recv()

    def left(buffer, units, semaphore):
        pltpu.make_async_remote_copy(
            src_ref=buffer.at[pl.ds(0, units)], dst_ref=buffer.at[pl.ds(0, units)], send_sem=semaphore,
            recv_sem=r1.at[0], device_id={"pz": q}, device_id_type=MESH,
        ).wait_send()

    def each_peer(action):
        def step(o, carry):
            action(lax.rem(q + o, NPZ))
            return carry

        lax.fori_loop(1, NPZ, step, 0)

    def start1(c, t, height):
        pltpu.make_async_remote_copy(
            src_ref=zt.at[pl.ds(16 * t + ZC * c, ZC), pl.ds(0, height), :],
            dst_ref=got1.at[pl.ds(ZC * c, ZC), pl.ds(pl.multiple_of(16 * q, 16), height), :],
            send_sem=send_sem.at[0],
            recv_sem=r1.at[c],
            device_id={"pz": t},
            device_id_type=MESH,
        ).start()

    @pl.when(full)
    def _():
        for c in range(CHUNKS):
            each_peer(lambda t: start1(c, t, 16))

    @pl.when(q == 6)
    def _():
        for c in range(CHUNKS):
            each_peer(lambda t: start1(c, t, 8))

    got1[:, pl.ds(pl.multiple_of(16 * q, 16), 16), :] = zt[pl.ds(16 * q, 16), :, :]

    def by_place(when_full, when_half, when_empty):
        pl.when(full)(when_full)
        pl.when(q == 6)(when_half)
        pl.when(jnp.logical_and(q > 6, q < 10))(when_empty)

    def wait1(c):
        by_place(
            lambda: arrived(zt, 11 * ZC + ZC // 2, r1.at[c]),
            lambda: arrived(zt, 12 * ZC, r1.at[c]),
            lambda: arrived(zt, 12 * ZC + ZC // 2, r1.at[c]),
        )

    def rows_pass(c, src, dst):
        z = ZC * c
        done = mm3(table(), split(jnp.concatenate([src[z], src[z + 1]], axis=1)))
        dst[z] = done[:, :128]
        dst[z + 1] = done[:, 128:]

    def start2(c, t):
        pltpu.make_async_remote_copy(
            src_ref=yt.at[pl.ds(ZC * c, ZC), pl.ds(pl.multiple_of(64 * t, 64), 64), :],
            dst_ref=got2.at[p, pl.ds(ZC * c, ZC), :, :],
            send_sem=send_sem.at[1],
            recv_sem=r2.at[c],
            device_id={"py": t},
            device_id_type=MESH,
        ).start()

    def send2(c):
        for o in (1, 3, 2):
            start2(c, lax.rem(p + o, NPY))

    def rows_step(c):
        wait1(c)
        rows_pass(c, got1, yt)
        got2[p, ZC * c : ZC * c + ZC] = yt[ZC * c : ZC * c + ZC, pl.ds(pl.multiple_of(64 * p, 64), 64), :]

    def wait_py(c, semaphore):
        pltpu.make_async_remote_copy(
            src_ref=got2.at[pl.ds(0, 3), pl.ds(0, ZC)], dst_ref=got2.at[pl.ds(0, 3), pl.ds(0, ZC)],
            send_sem=send_sem.at[1], recv_sem=semaphore, device_id={"py": p}, device_id_type=MESH,
        ).wait_recv()

    lower = iota((ROWS, 128), 1) < 64

    def swap(values):
        return pltpu.roll(values, 64, 1)

    def width_step(c):
        wait_py(c, r2.at[c])
        part = [got2[k, ZC * c : ZC * c + ZC].reshape(ROWS, 128) for k in range(NPY)]
        turned = [swap(value) for value in part]
        first = [jnp.where(lower, part[k], turned[k + 1]) for k in (0, 2)]
        second = [jnp.where(lower, turned[k], part[k + 1]) for k in (0, 2)]
        lines = jnp.concatenate([jnp.concatenate(first, axis=1), jnp.concatenate(second, axis=1)], axis=0)
        real = mm3(split(lines), table())
        field[ROWS * c : ROWS * c + ROWS, :GRID] = real[:ROWS]
        field[ROWS * c : ROWS * c + ROWS, GRID:] = real[ROWS:]

    def gather(c0, c1):
        high, low = split(field[ROWS * c0 : ROWS * c1, :])
        hot = cols_hot[:, ROWS * c0 : ROWS * c1]
        part = mm(hot, high) + mm(hot, low)
        if c0 == 0:
            gathered[...] = part
        else:
            gathered[...] += part

    def one_hot_tables():
        block_row = block[...]
        row_of = lax.shift_right_logical(block_row, 1)
        for k in range(8):
            hot = iota((128, ENT), 0) + 128 * k == jnp.broadcast_to(row_of, (128, ENT))
            rows_hot[128 * k : 128 * k + 128, :] = jnp.where(hot, 1.0, 0.0).astype(BF16)

        eye = iota((ENT, ENT), 0) == iota((ENT, ENT), 1)

        def to_column(row):
            diag = jnp.where(eye, jnp.broadcast_to(row.astype(F32), (ENT, ENT)), 0.0)
            return mm(diag.astype(BF16), jnp.ones((ENT, 128), BF16))

        row_col = 32.0 * to_column(lax.shift_right_logical(row_of, 5)) + to_column(row_of & 31)
        for k in range(8):
            hot = (iota((ENT, 128), 1) + 128 * k).astype(F32) == row_col
            cols_hot[:, 128 * k : 128 * k + 128] = jnp.where(hot, 1.0, 0.0).astype(BF16)
        parity[...] = to_column(block_row & 1)

        atoms = atom[...]
        owner = lax.shift_right_logical(atoms, 6)
        dp = (lax.shift_right_logical(owner, 4) - p) & 3
        dq = ((owner & 15) - q) & 15
        slot = jnp.where(dp == 3, 1, jnp.where(dp == 1, 2, jnp.where(dq == 15, 3, jnp.where(dq == 1, 4, 0))))
        code = slot * 64 + (atoms & 63)
        hot = iota((320, ENT), 0) == jnp.broadcast_to(code, (320, ENT))
        atom_hot[...] = jnp.where(hot, 1.0, 0.0).astype(BF16)

    proj_rows = proj.reshape(ENT * 8, 128)
    lane = iota((ENT, 128), 1)

    def neighbour(s):
        if s < 3:
            return {"py": lax.rem(p + (3 if s == 1 else 1), NPY)}
        return {"pz": lax.rem(q + (15 if s == 3 else 1), NPZ)}

    def copy_terms(rnd, s):
        return pltpu.make_async_remote_copy(
            src_ref=terms.at[rnd, s], dst_ref=terms_in.at[rnd, OPPOSITE[s]], send_sem=st.at[rnd, s],
            recv_sem=rt.at[rnd, OPPOSITE[s]], device_id=neighbour(s), device_id_type=MESH,
        )

    def copy_coupled(rnd, s):
        return pltpu.make_async_remote_copy(
            src_ref=coupled.at[rnd, 0], dst_ref=coupled.at[rnd, OPPOSITE[s]], send_sem=sc.at[rnd, s],
            recv_sem=rc.at[rnd, OPPOSITE[s]], device_id=neighbour(s), device_id_type=MESH,
        )

    def send_terms(rnd):
        odd = parity[...] > 0.5
        entry_terms = jnp.zeros((ENT, 128), F32)
        if rnd == 0:
            whole = gathered[...]
        else:
            high, low = split(field[ROWS * 5 :, :])
            hot = cols_hot[:, ROWS * 5 :]
            whole = gathered[...] + (mm(hot, high) + mm(hot, low))
        for n in range(2):
            cells = jnp.where(odd, whole[:, 256 * n + 128 : 256 * n + 256], whole[:, 256 * n : 256 * n + 128])
            for i in range(8):
                high, low = split(proj_rows[pl.ds(i, ENT, stride=8), :] * cells)
                sums = mm(jnp.concatenate([high, low], axis=1), jnp.ones((256, 128), BF16))
                entry_terms = jnp.where(lane == 8 * n + i, sums, entry_terms)
        high, low = split(entry_terms)
        hot = atom_hot[...]
        terms[rnd] = (mm(hot, high) + mm(hot, low)).reshape(5, 64, 128)
        for s in range(1, 5):
            copy_terms(rnd, s).start()

    def send_coupled(rnd):
        symmetric = 0.5 * (coupling[...] + coupling[...].T)
        place = jnp.where((iota((128, 8), 0) & 7) == iota((128, 8), 1), 1.0, 0.0)
        tiled = jnp.dot(jnp.dot(place, symmetric, precision=HIGHEST), place.T, precision=HIGHEST)
        same = lax.shift_right_logical(iota((128, 128), 0), 3) == lax.shift_right_logical(iota((128, 128), 1), 3)
        mix = jnp.where(same, tiled, 0.0)
        total = terms[rnd, 0]
        for s in range(1, 5):
            copy_terms(rnd, OPPOSITE[s]).wait_recv()
            total = total + terms_in[rnd, s]
        coupled[rnd, 0] = jnp.dot(total, mix, precision=HIGHEST)
        for s in range(1, 5):
            copy_coupled(rnd, s).start()

    def spread_coupled(rnd):
        for s in range(1, 5):
            copy_coupled(rnd, OPPOSITE[s]).wait_recv()
        odd = parity[...]
        hot = atom_hot[...]
        high, low = split(coupled[rnd].reshape(320, 128))
        chosen = mm(hot, high, TN) + mm(hot, low, TN)
        for n in range(2):
            cells = jnp.zeros((ENT, 128), F32)
            for i in range(8):
                j = 8 * n + i
                weight = jnp.broadcast_to(chosen[:, j : j + 1], (ENT, 128))
                cells += proj_rows[pl.ds(i, ENT, stride=8), :] * weight
            for half in range(2):
                high, low = split(jnp.where(odd > 0.5, cells if half else 0.0, 0.0 if half else cells))
                lanes = slice(256 * n + 128 * half, 256 * n + 128 * half + 128)
                spread_hi[:, lanes] = high
                spread_lo[:, lanes] = low

    def start3(c, t):
        pltpu.make_async_remote_copy(
            src_ref=xb.at[t, pl.ds(ZC * c, ZC), :, :],
            dst_ref=got3.at[pl.ds(ZC * c, ZC), pl.ds(pl.multiple_of(64 * p, 64), 64), :],
            send_sem=send_sem.at[2],
            recv_sem=r3.at[c],
            device_id={"py": t},
            device_id_type=MESH,
        ).start()

    def send3(c):
        for o in (1, 3, 2):
            start3(c, lax.rem(p + o, NPY))

    def back_step(c0, c1):
        rows = slice(ROWS * c0, ROWS * c1)
        hot = rows_hot[rows, :]
        placed = mm(hot, spread_hi[...]) + mm(hot, spread_lo[...])
        count = ROWS * (c1 - c0)
        local = pot[ZC * c0 : ZC * c1].reshape(count, GRID)
        whole = [local * field[rows, GRID * n : GRID * n + GRID] + placed[:, GRID * n : GRID * n + GRID] for n in range(2)]
        done = mm3(split(jnp.concatenate(whole, axis=0)), table())
        for c in range(c0, c1):
            top = ROWS * (c - c0)
            for h in range(2):
                first = done[top : top + ROWS, 128 * h : 128 * h + 128]
                second = done[count + top : count + top + ROWS, 128 * h : 128 * h + 128]
                xb[2 * h, ZC * c : ZC * c + ZC] = jnp.where(lower, first, swap(second)).reshape(ZC, 64, 128)
                xb[2 * h + 1, ZC * c : ZC * c + ZC] = jnp.where(lower, swap(first), second).reshape(ZC, 64, 128)
            got3[ZC * c : ZC * c + ZC, pl.ds(pl.multiple_of(64 * p, 64), 64), :] = xb[p, ZC * c : ZC * c + ZC]

    def start4(c, t, height):
        pltpu.make_async_remote_copy(
            src_ref=yb.at[pl.ds(ZC * c, ZC), pl.ds(pl.multiple_of(16 * t, 16), height), :],
            dst_ref=got4.at[pl.ds(16 * q + ZC * c, ZC), pl.ds(0, height), :],
            send_sem=send_sem.at[3],
            recv_sem=r4,
            device_id={"pz": t},
            device_id_type=MESH,
        ).start()

    def final_rows(c):
        wait_py(c, r3.at[c])
        rows_pass(c, got3, yb)

    def send4(c):
        def one(t):
            @pl.when(jnp.logical_or(t < 6, t > 9))
            def _():
                start4(c, t, 16)

            @pl.when(t == 6)
            def _():
                start4(c, t, 8)

        each_peer(one)

    apart(one_hot_tables)
    for c in range(CHUNKS):
        apart(functools.partial(rows_step, c))
        if c < 2:
            send2(c)
    for load in loads:
        load.wait()
    apart(functools.partial(width_step, 0))
    send2(2)
    apart(functools.partial(width_step, 1))
    send2(3)
    apart(functools.partial(gather, 0, 2))
    apart(functools.partial(width_step, 2))
    send2(4)
    apart(functools.partial(width_step, 3))
    send2(5)
    apart(functools.partial(gather, 2, 4))
    apart(functools.partial(width_step, 4))
    apart(functools.partial(gather, 4, 5))
    apart(functools.partial(send_terms, 0))
    send2(6)
    apart(functools.partial(width_step, 5))
    apart(functools.partial(send_coupled, 0))
    send2(7)
    apart(functools.partial(width_step, 6))
    apart(functools.partial(spread_coupled, 0))
    apart(functools.partial(back_step, 1, 2))
    send3(1)
    apart(functools.partial(width_step, 7))
    apart(functools.partial(send_terms, 1))
    apart(functools.partial(back_step, 2, 4))
    send3(2)
    apart(functools.partial(final_rows, 1))
    apart(functools.partial(send_coupled, 1))
    send3(3)
    send4(1)
    apart(functools.partial(final_rows, 2))
    apart(functools.partial(spread_coupled, 1))
    apart(functools.partial(back_step, 4, 6))
    send3(4)
    send3(5)
    send4(2)
    apart(functools.partial(back_step, 6, 8))
    apart(functools.partial(back_step, 0, 1))
    apart(functools.partial(final_rows, 3))
    send3(6)
    send4(3)
    apart(functools.partial(final_rows, 4))
    send3(7)
    send4(4)
    apart(functools.partial(final_rows, 5))
    send3(0)
    send4(5)
    apart(functools.partial(final_rows, 6))
    send4(6)
    apart(functools.partial(final_rows, 7))
    send4(7)
    apart(functools.partial(final_rows, 0))
    send4(0)
    own = pltpu.make_async_copy(
        yb.at[:, pl.ds(pl.multiple_of(16 * q, 16), 16), :], got4.at[pl.ds(16 * q, 16), :, :], local_sem.at[2]
    )
    own.start()

    pl.when(full)(lambda: left(zt, 15 * 16, send_sem.at[0]))
    pl.when(q == 6)(lambda: left(zt, 15 * 8, send_sem.at[0]))
    for k in (1, 2):
        pltpu.make_async_remote_copy(
            src_ref=got2.at[pl.ds(0, 3)], dst_ref=got2.at[pl.ds(0, 3)], send_sem=send_sem.at[k], recv_sem=r2.at[0],
            device_id={"py": p}, device_id_type=MESH,
        ).wait_send()
    for rnd in range(2):
        for s in range(1, 5):
            copy_terms(rnd, s).wait_send()
            copy_coupled(rnd, s).wait_send()

    pl.when(full)(lambda: arrived(zt, 15 * 16, r4))
    pl.when(q == 6)(lambda: arrived(zt, 15 * 8, r4))

    by_place(
        lambda: left(zt, 11 * 16 + 8, send_sem.at[3]),
        lambda: left(zt, 12 * 16, send_sem.at[3]),
        lambda: left(zt, 12 * 16 + 8, send_sem.at[3]),
    )
    own.wait()


def finish(limit, chi, clo, got4, coef, out):
    p = lax.axis_index("py")
    q = lax.axis_index("pz")
    base = 8 * pl.program_id(0)
    rows = got4.reshape(2048, 128)

    def final_step(y, carry):
        keep = inside(limit, base + y)
        lines = rows[pl.ds(y, GRID, stride=8), :]
        done = mm3(split(lines), (chi[...], clo[...]), TN)
        fy = freq(16 * q + base + y)
        fx = freq(64 * p + iota((64, GRID), 0))
        fz = freq(iota((64, GRID), 1))
        kinetic = (fz * fz + fx * fx + fy * fy).astype(F32) * (0.5 * (4.0 / GRID) ** 2)
        for n in range(2):
            out[n, y] = jnp.where(keep, kinetic * coef[n, y] + done[64 * n : 64 * n + 64, :], 0.0)
        return carry

    lax.fori_loop(0, 8, final_step, 0, unroll=8)


def shards(coefficients, potential, column_limit, entry_atom, entry_block, projectors, coupling):
    vmem = pl.BlockSpec(memory_space=pltpu.VMEM)
    anywhere = pl.BlockSpec(memory_space=pl.ANY)
    big = pltpu.VMEM((16, 256, 128), F32)
    dma = pltpu.SemaphoreType.DMA
    cas = [jnp.asarray(table) for table in halves(cas_matrix())]
    columns = pl.pallas_call(
        kernel,
        name="hamiltonian",
        out_shape=jax.ShapeDtypeStruct((256, 16, 128), F32),
        in_specs=[vmem] * 6 + [anywhere] * 3,
        out_specs=anywhere,
        scratch_shapes=[
            pltpu.VMEM((2, 16, 64, GRID), F32),
            pltpu.VMEM((16, 64, GRID), F32),
            pltpu.VMEM((ENT, 8, 128), F32),
            pltpu.VMEM((256, 16, 128), F32),
            big,
            big,
            pltpu.VMEM((NPY, 16, 64, 128), F32),
            pltpu.VMEM((1024, 512), F32),
            pltpu.VMEM((NPY, 16, 64, 128), F32),
            big,
            big,
            pltpu.VMEM((1024, ENT), BF16),
            pltpu.VMEM((ENT, 1024), BF16),
            pltpu.VMEM((ENT, 128), F32),
            pltpu.VMEM((320, ENT), BF16),
            pltpu.VMEM((ENT, 512), F32),
            pltpu.VMEM((ENT, 512), BF16),
            pltpu.VMEM((ENT, 512), BF16),
            pltpu.VMEM((2, 5, 64, 128), F32),
            pltpu.VMEM((2, 5, 64, 128), F32),
            pltpu.VMEM((2, 5, 64, 128), F32),
            dma((3,)),
            dma((4,)),
            dma((4,)),
            dma((CHUNKS,)),
            dma((CHUNKS,)),
            dma((CHUNKS,)),
            dma,
            dma((2, 5)),
            dma((2, 5)),
            dma((2, 5)),
            dma((2, 5)),
        ],
        compiler_params=pltpu.CompilerParams(
            collective_id=0, has_side_effects=True, vmem_limit_bytes=56 * 2**20
        ),
    )(
        column_limit,
        entry_atom.reshape(1, ENT),
        entry_block.reshape(1, ENT),
        coupling,
        *cas,
        coefficients,
        potential,
        projectors,
    )
    whole = pl.BlockSpec((16, 64), lambda g: (0, 0))
    square = pl.BlockSpec((GRID, GRID), lambda g: (0, 0))
    bands = pl.BlockSpec((2, 8, 64, GRID), lambda g: (0, g, 0, 0))
    return pl.pallas_call(
        finish,
        name="finish",
        grid=(2,),
        out_shape=jax.ShapeDtypeStruct(coefficients.shape, F32),
        in_specs=[whole, square, square, pl.BlockSpec((256, 8, 128), lambda g: (0, g, 0)), bands],
        out_specs=bands,
        compiler_params=pltpu.CompilerParams(vmem_limit_bytes=60 * 2**20),
    )(column_limit, *cas, columns, coefficients)


def solution(mesh):
    in_specs = (
        P("band", "pz", "py", None),
        P("pz", "py", None),
        P("pz", "py"),
        P(("py", "pz"), None),
        P(("py", "pz")),
        P(("py", "pz"), None, None),
        P(),
    )
    out_specs = P("band", "pz", "py", None)
    return jax.shard_map(shards, mesh=mesh, in_specs=in_specs, out_specs=out_specs, check_vma=False)
```

```python
import functools
import math

import jax
import jax.numpy as jnp
import numpy as np
from jax import lax
from jax.experimental import pallas as pl
from jax.experimental.pallas import tpu as pltpu
from jax.sharding import PartitionSpec as P

F32 = jnp.float32
BF16 = jnp.bfloat16
I32 = jnp.int32
MESH = pl.DeviceIdType.MESH
HIGHEST = lax.Precision.HIGHEST

NPY, NPZ = 4, 16
GRID = 256
CHUNKS = 8
ZC = 2
ROWS = 64 * ZC
ENT = 512
OPPOSITE = (0, 2, 1, 4, 3)


def cas_matrix():
    index = np.arange(GRID)
    angle = (index[:, None] * index[None, :] % GRID) * (2.0 * math.pi / GRID)
    return ((np.cos(angle) + np.sin(angle)) / math.sqrt(GRID)).astype(np.float32)


def halves(table):
    high = table.astype(jnp.bfloat16)
    low = (table - high.astype(np.float32)).astype(jnp.bfloat16)
    return high, low


def split(values):
    high = values.astype(BF16)
    return high, (values - high.astype(F32)).astype(BF16)


NN = (((1,), (0,)), ((), ()))
NT = (((1,), (1,)), ((), ()))
TN = (((0,), (0,)), ((), ()))


def mm(a, b, dims=NN):
    return lax.dot_general(a, b, dims, preferred_element_type=F32)


def mm3(a, b, dims=NN):
    (a_high, a_low), (b_high, b_low) = a, b
    return mm(a_high, b_high, dims) + (mm(a_high, b_low, dims) + mm(a_low, b_high, dims))


def iota(shape, dim):
    return lax.broadcasted_iota(I32, shape, dim)


def freq(index):
    return jnp.minimum(index, GRID - index)


def inside(limit, y):
    row = limit[pl.ds(y, 1), :].astype(F32)
    diag = jnp.where(iota((64, 64), 0) == iota((64, 64), 1), jnp.broadcast_to(row, (64, 64)), 0.0)
    bound = mm(diag.astype(BF16), jnp.ones((64, GRID), BF16))
    return freq(iota((64, GRID), 1)).astype(F32) <= bound


def kernel(
    limit, atom, block, coupling, chi, clo, coef_any, pot_any, proj_any,
    got4,
    coef, pot, proj,
    zt, got1, yt, got2, field, xb, got3, yb,
    rows_hot, cols_hot, parity, atom_hot, gathered, spread_hi, spread_lo, terms, terms_in, coupled,
    local_sem, coef_sem, send_sem, r1, r2, r3, r4, st, rt, sc, rc,
):
    p = lax.axis_index("py")
    q = lax.axis_index("pz")
    full = jnp.logical_or(q < 6, q > 9)

    coef_loads = [
        pltpu.make_async_copy(coef_any.at[:, 4 * k : 4 * k + 4], coef.at[:, 4 * k : 4 * k + 4], coef_sem.at[k])
        for k in range(4)
    ]
    loads = [
        pltpu.make_async_copy(proj_any, proj, local_sem.at[0]),
        pltpu.make_async_copy(pot_any, pot, local_sem.at[1]),
    ]
    for load in coef_loads + loads:
        load.start()

    got1[:, 96:160, :] = jnp.zeros((16, 64, 128), F32)

    barrier = pltpu.get_barrier_semaphore()
    for o in range(1, NPZ):
        pl.semaphore_signal(barrier, inc=1, device_id={"pz": lax.rem(q + o, NPZ)}, device_id_type=MESH)
    for o in range(1, NPY):
        pl.semaphore_signal(barrier, inc=1, device_id={"py": lax.rem(p + o, NPY)}, device_id_type=MESH)

    def table():
        return chi[...], clo[...]

    def apart(work):
        pl.when(q >= 0)(work)

    zt_rows = zt.reshape(4096, 128)

    def depth_step(y, carry):
        keep = inside(limit, y)
        pair = jnp.concatenate([jnp.where(keep, coef[0, y], 0.0), jnp.where(keep, coef[1, y], 0.0)], axis=0)
        zt_rows[pl.ds(y, GRID, stride=16), :] = mm3(table(), split(pair), NT)
        return carry

    for k in range(4):
        coef_loads[k].wait()
        lax.fori_loop(4 * k, 4 * k + 4, depth_step, 0, unroll=4)

    pl.semaphore_wait(barrier, NPZ + NPY - 2)

    def arrived(buffer, units, semaphore):
        pltpu.make_async_remote_copy(
            src_ref=buffer.at[pl.ds(0, units)], dst_ref=buffer.at[pl.ds(0, units)], send_sem=send_sem.at[0],
            recv_sem=semaphore, device_id={"pz": q}, device_id_type=MESH,
        ).wait_recv()

    def left(buffer, units, semaphore):
        pltpu.make_async_remote_copy(
            src_ref=buffer.at[pl.ds(0, units)], dst_ref=buffer.at[pl.ds(0, units)], send_sem=semaphore,
            recv_sem=r1.at[0], device_id={"pz": q}, device_id_type=MESH,
        ).wait_send()

    def each_peer(action):
        def step(o, carry):
            action(lax.rem(q + o, NPZ))
            return carry

        lax.fori_loop(1, NPZ, step, 0)

    def start1(c, t, height):
        pltpu.make_async_remote_copy(
            src_ref=zt.at[pl.ds(16 * t + ZC * c, ZC), pl.ds(0, height), :],
            dst_ref=got1.at[pl.ds(ZC * c, ZC), pl.ds(pl.multiple_of(16 * q, 16), height), :],
            send_sem=send_sem.at[0],
            recv_sem=r1.at[c],
            device_id={"pz": t},
            device_id_type=MESH,
        ).start()

    @pl.when(full)
    def _():
        for c in range(CHUNKS):
            each_peer(lambda t: start1(c, t, 16))

    @pl.when(q == 6)
    def _():
        for c in range(CHUNKS):
            each_peer(lambda t: start1(c, t, 8))

    got1[:, pl.ds(pl.multiple_of(16 * q, 16), 16), :] = zt[pl.ds(16 * q, 16), :, :]

    def by_place(when_full, when_half, when_empty):
        pl.when(full)(when_full)
        pl.when(q == 6)(when_half)
        pl.when(jnp.logical_and(q > 6, q < 10))(when_empty)

    def wait1(c):
        by_place(
            lambda: arrived(zt, 11 * ZC + ZC // 2, r1.at[c]),
            lambda: arrived(zt, 12 * ZC, r1.at[c]),
            lambda: arrived(zt, 12 * ZC + ZC // 2, r1.at[c]),
        )

    def rows_pass(c, src, dst):
        z = ZC * c
        done = mm3(table(), split(jnp.concatenate([src[z], src[z + 1]], axis=1)))
        dst[z] = done[:, :128]
        dst[z + 1] = done[:, 128:]

    def start2(c, t):
        pltpu.make_async_remote_copy(
            src_ref=yt.at[pl.ds(ZC * c, ZC), pl.ds(pl.multiple_of(64 * t, 64), 64), :],
            dst_ref=got2.at[p, pl.ds(ZC * c, ZC), :, :],
            send_sem=send_sem.at[1],
            recv_sem=r2.at[c],
            device_id={"py": t},
            device_id_type=MESH,
        ).start()

    def send2(c):
        for o in (1, 3, 2):
            start2(c, lax.rem(p + o, NPY))

    def rows_step(c):
        wait1(c)
        rows_pass(c, got1, yt)
        got2[p, ZC * c : ZC * c + ZC] = yt[ZC * c : ZC * c + ZC, pl.ds(pl.multiple_of(64 * p, 64), 64), :]

    def wait_py(c, semaphore):
        pltpu.make_async_remote_copy(
            src_ref=got2.at[pl.ds(0, 3), pl.ds(0, ZC)], dst_ref=got2.at[pl.ds(0, 3), pl.ds(0, ZC)],
            send_sem=send_sem.at[1], recv_sem=semaphore, device_id={"py": p}, device_id_type=MESH,
        ).wait_recv()

    lower = iota((ROWS, 128), 1) < 64

    def swap(values):
        return pltpu.roll(values, 64, 1)

    def width_step(c):
        wait_py(c, r2.at[c])
        part = [got2[k, ZC * c : ZC * c + ZC].reshape(ROWS, 128) for k in range(NPY)]
        turned = [swap(value) for value in part]
        first = [jnp.where(lower, part[k], turned[k + 1]) for k in (0, 2)]
        second = [jnp.where(lower, turned[k], part[k + 1]) for k in (0, 2)]
        lines = jnp.concatenate([jnp.concatenate(first, axis=1), jnp.concatenate(second, axis=1)], axis=0)
        real = mm3(split(lines), table())
        field[ROWS * c : ROWS * c + ROWS, :GRID] = real[:ROWS]
        field[ROWS * c : ROWS * c + ROWS, GRID:] = real[ROWS:]

    def gather(c0, c1):
        high, low = split(field[ROWS * c0 : ROWS * c1, :])
        hot = cols_hot[:, ROWS * c0 : ROWS * c1]
        part = mm(hot, high) + mm(hot, low)
        if c0 == 0:
            gathered[...] = part
        else:
            gathered[...] += part

    def one_hot_tables():
        block_row = block[...]
        row_of = lax.shift_right_logical(block_row, 1)
        for k in range(8):
            hot = iota((128, ENT), 0) + 128 * k == jnp.broadcast_to(row_of, (128, ENT))
            rows_hot[128 * k : 128 * k + 128, :] = jnp.where(hot, 1.0, 0.0).astype(BF16)

        eye = iota((ENT, ENT), 0) == iota((ENT, ENT), 1)

        def to_column(row):
            diag = jnp.where(eye, jnp.broadcast_to(row.astype(F32), (ENT, ENT)), 0.0)
            return mm(diag.astype(BF16), jnp.ones((ENT, 128), BF16))

        row_col = 32.0 * to_column(lax.shift_right_logical(row_of, 5)) + to_column(row_of & 31)
        for k in range(8):
            hot = (iota((ENT, 128), 1) + 128 * k).astype(F32) == row_col
            cols_hot[:, 128 * k : 128 * k + 128] = jnp.where(hot, 1.0, 0.0).astype(BF16)
        parity[...] = to_column(block_row & 1)

        atoms = atom[...]
        owner = lax.shift_right_logical(atoms, 6)
        dp = (lax.shift_right_logical(owner, 4) - p) & 3
        dq = ((owner & 15) - q) & 15
        slot = jnp.where(dp == 3, 1, jnp.where(dp == 1, 2, jnp.where(dq == 15, 3, jnp.where(dq == 1, 4, 0))))
        code = slot * 64 + (atoms & 63)
        hot = iota((320, ENT), 0) == jnp.broadcast_to(code, (320, ENT))
        atom_hot[...] = jnp.where(hot, 1.0, 0.0).astype(BF16)

    proj_rows = proj.reshape(ENT * 8, 128)
    lane = iota((ENT, 128), 1)

    def neighbour(s):
        if s < 3:
            return {"py": lax.rem(p + (3 if s == 1 else 1), NPY)}
        return {"pz": lax.rem(q + (15 if s == 3 else 1), NPZ)}

    def copy_terms(rnd, s):
        return pltpu.make_async_remote_copy(
            src_ref=terms.at[rnd, s], dst_ref=terms_in.at[rnd, OPPOSITE[s]], send_sem=st.at[rnd, s],
            recv_sem=rt.at[rnd, OPPOSITE[s]], device_id=neighbour(s), device_id_type=MESH,
        )

    def copy_coupled(rnd, s):
        return pltpu.make_async_remote_copy(
            src_ref=coupled.at[rnd, 0], dst_ref=coupled.at[rnd, OPPOSITE[s]], send_sem=sc.at[rnd, s],
            recv_sem=rc.at[rnd, OPPOSITE[s]], device_id=neighbour(s), device_id_type=MESH,
        )

    def send_terms(rnd):
        odd = parity[...] > 0.5
        entry_terms = jnp.zeros((ENT, 128), F32)
        if rnd == 0:
            whole = gathered[...]
        else:
            high, low = split(field[ROWS * 5 :, :])
            hot = cols_hot[:, ROWS * 5 :]
            whole = gathered[...] + (mm(hot, high) + mm(hot, low))
        for n in range(2):
            cells = jnp.where(odd, whole[:, 256 * n + 128 : 256 * n + 256], whole[:, 256 * n : 256 * n + 128])
            for i in range(8):
                high, low = split(proj_rows[pl.ds(i, ENT, stride=8), :] * cells)
                sums = mm(jnp.concatenate([high, low], axis=1), jnp.ones((256, 128), BF16))
                entry_terms = jnp.where(lane == 8 * n + i, sums, entry_terms)
        high, low = split(entry_terms)
        hot = atom_hot[...]
        sums = mm(hot, high) + mm(hot, low)
        for s in range(5):
            square = jnp.concatenate([sums[64 * s : 64 * s + 64], jnp.zeros((64, 128), F32)], axis=0)
            terms[rnd, s] = square.T[:16]
        for s in range(1, 5):
            copy_terms(rnd, s).start()

    def send_coupled(rnd):
        symmetric = 0.5 * (coupling[...] + coupling[...].T)
        place = jnp.where((iota((16, 8), 0) & 7) == iota((16, 8), 1), 1.0, 0.0)
        tiled = jnp.dot(jnp.dot(place, symmetric, precision=HIGHEST), place.T, precision=HIGHEST)
        same = lax.shift_right_logical(iota((16, 16), 0), 3) == lax.shift_right_logical(iota((16, 16), 1), 3)
        mix = jnp.where(same, tiled, 0.0)
        total = terms[rnd, 0]
        for s in range(1, 5):
            copy_terms(rnd, OPPOSITE[s]).wait_recv()
            total = total + terms_in[rnd, s]
        coupled[rnd, 0] = jnp.dot(mix, total, precision=HIGHEST)
        for s in range(1, 5):
            copy_coupled(rnd, s).start()

    def spread_coupled(rnd):
        for s in range(1, 5):
            copy_coupled(rnd, OPPOSITE[s]).wait_recv()
        odd = parity[...]
        hot = atom_hot[...]
        filler = jnp.zeros((112, 128), F32)
        squares = [jnp.concatenate([coupled[rnd, s], filler], axis=0).T[:64] for s in range(5)]
        high, low = split(jnp.concatenate(squares, axis=0))
        chosen = mm(hot, high, TN) + mm(hot, low, TN)
        for n in range(2):
            cells = jnp.zeros((ENT, 128), F32)
            for i in range(8):
                j = 8 * n + i
                weight = jnp.broadcast_to(chosen[:, j : j + 1], (ENT, 128))
                cells += proj_rows[pl.ds(i, ENT, stride=8), :] * weight
            for half in range(2):
                high, low = split(jnp.where(odd > 0.5, cells if half else 0.0, 0.0 if half else cells))
                lanes = slice(256 * n + 128 * half, 256 * n + 128 * half + 128)
                spread_hi[:, lanes] = high
                spread_lo[:, lanes] = low

    def start3(c, t):
        pltpu.make_async_remote_copy(
            src_ref=xb.at[t, pl.ds(ZC * c, ZC), :, :],
            dst_ref=got3.at[pl.ds(ZC * c, ZC), pl.ds(pl.multiple_of(64 * p, 64), 64), :],
            send_sem=send_sem.at[2],
            recv_sem=r3.at[c],
            device_id={"py": t},
            device_id_type=MESH,
        ).start()

    def send3(c):
        for o in (1, 3, 2):
            start3(c, lax.rem(p + o, NPY))

    def back_step(c0, c1):
        rows = slice(ROWS * c0, ROWS * c1)
        hot = rows_hot[rows, :]
        placed = mm(hot, spread_hi[...]) + mm(hot, spread_lo[...])
        count = ROWS * (c1 - c0)
        local = pot[ZC * c0 : ZC * c1].reshape(count, GRID)
        whole = [local * field[rows, GRID * n : GRID * n + GRID] + placed[:, GRID * n : GRID * n + GRID] for n in range(2)]
        done = mm3(split(jnp.concatenate(whole, axis=0)), table())
        for c in range(c0, c1):
            top = ROWS * (c - c0)
            for h in range(2):
                first = done[top : top + ROWS, 128 * h : 128 * h + 128]
                second = done[count + top : count + top + ROWS, 128 * h : 128 * h + 128]
                xb[2 * h, ZC * c : ZC * c + ZC] = jnp.where(lower, first, swap(second)).reshape(ZC, 64, 128)
                xb[2 * h + 1, ZC * c : ZC * c + ZC] = jnp.where(lower, swap(first), second).reshape(ZC, 64, 128)
            got3[ZC * c : ZC * c + ZC, pl.ds(pl.multiple_of(64 * p, 64), 64), :] = xb[p, ZC * c : ZC * c + ZC]

    def start4(c, t, height):
        pltpu.make_async_remote_copy(
            src_ref=yb.at[pl.ds(ZC * c, ZC), pl.ds(pl.multiple_of(16 * t, 16), height), :],
            dst_ref=got4.at[pl.ds(16 * q + ZC * c, ZC), pl.ds(0, height), :],
            send_sem=send_sem.at[3],
            recv_sem=r4,
            device_id={"pz": t},
            device_id_type=MESH,
        ).start()

    def final_rows(c):
        wait_py(c, r3.at[c])
        rows_pass(c, got3, yb)

    def send4(c):
        def one(t):
            @pl.when(jnp.logical_or(t < 6, t > 9))
            def _():
                start4(c, t, 16)

            @pl.when(t == 6)
            def _():
                start4(c, t, 8)

        each_peer(one)

    apart(one_hot_tables)
    for c in range(CHUNKS):
        apart(functools.partial(rows_step, c))
        if c < 2:
            send2(c)
    for load in loads:
        load.wait()
    apart(functools.partial(width_step, 0))
    send2(2)
    apart(functools.partial(width_step, 1))
    send2(3)
    apart(functools.partial(gather, 0, 2))
    apart(functools.partial(width_step, 2))
    send2(4)
    apart(functools.partial(width_step, 3))
    send2(5)
    apart(functools.partial(gather, 2, 4))
    apart(functools.partial(width_step, 4))
    apart(functools.partial(gather, 4, 5))
    apart(functools.partial(send_terms, 0))
    send2(6)
    apart(functools.partial(width_step, 5))
    apart(functools.partial(send_coupled, 0))
    send2(7)
    apart(functools.partial(width_step, 6))
    apart(functools.partial(spread_coupled, 0))
    apart(functools.partial(back_step, 1, 2))
    send3(1)
    apart(functools.partial(width_step, 7))
    apart(functools.partial(send_terms, 1))
    apart(functools.partial(back_step, 2, 4))
    send3(2)
    apart(functools.partial(final_rows, 1))
    apart(functools.partial(send_coupled, 1))
    send3(3)
    send4(1)
    apart(functools.partial(final_rows, 2))
    apart(functools.partial(spread_coupled, 1))
    apart(functools.partial(back_step, 4, 6))
    send3(4)
    send3(5)
    send4(2)
    apart(functools.partial(back_step, 6, 8))
    apart(functools.partial(back_step, 0, 1))
    apart(functools.partial(final_rows, 3))
    send3(6)
    send4(3)
    apart(functools.partial(final_rows, 4))
    send3(7)
    send4(4)
    apart(functools.partial(final_rows, 5))
    send3(0)
    send4(5)
    apart(functools.partial(final_rows, 6))
    send4(6)
    apart(functools.partial(final_rows, 7))
    send4(7)
    apart(functools.partial(final_rows, 0))
    send4(0)
    own = pltpu.make_async_copy(
        yb.at[:, pl.ds(pl.multiple_of(16 * q, 16), 16), :], got4.at[pl.ds(16 * q, 16), :, :], local_sem.at[2]
    )
    own.start()

    pl.when(full)(lambda: left(zt, 15 * 16, send_sem.at[0]))
    pl.when(q == 6)(lambda: left(zt, 15 * 8, send_sem.at[0]))
    for k in (1, 2):
        pltpu.make_async_remote_copy(
            src_ref=got2.at[pl.ds(0, 3)], dst_ref=got2.at[pl.ds(0, 3)], send_sem=send_sem.at[k], recv_sem=r2.at[0],
            device_id={"py": p}, device_id_type=MESH,
        ).wait_send()
    for rnd in range(2):
        for s in range(1, 5):
            copy_terms(rnd, s).wait_send()
            copy_coupled(rnd, s).wait_send()

    pl.when(full)(lambda: arrived(zt, 15 * 16, r4))
    pl.when(q == 6)(lambda: arrived(zt, 15 * 8, r4))

    by_place(
        lambda: left(zt, 11 * 16 + 8, send_sem.at[3]),
        lambda: left(zt, 12 * 16, send_sem.at[3]),
        lambda: left(zt, 12 * 16 + 8, send_sem.at[3]),
    )
    own.wait()


def finish(limit, chi, clo, got4, coef, out):
    p = lax.axis_index("py")
    q = lax.axis_index("pz")
    base = 8 * pl.program_id(0)
    rows = got4.reshape(2048, 128)

    def final_step(y, carry):
        keep = inside(limit, base + y)
        lines = rows[pl.ds(y, GRID, stride=8), :]
        done = mm3(split(lines), (chi[...], clo[...]), TN)
        fy = freq(16 * q + base + y)
        fx = freq(64 * p + iota((64, GRID), 0))
        fz = freq(iota((64, GRID), 1))
        kinetic = (fz * fz + fx * fx + fy * fy).astype(F32) * (0.5 * (4.0 / GRID) ** 2)
        for n in range(2):
            out[n, y] = jnp.where(keep, kinetic * coef[n, y] + done[64 * n : 64 * n + 64, :], 0.0)
        return carry

    lax.fori_loop(0, 8, final_step, 0, unroll=8)


def shards(coefficients, potential, column_limit, entry_atom, entry_block, projectors, coupling):
    vmem = pl.BlockSpec(memory_space=pltpu.VMEM)
    anywhere = pl.BlockSpec(memory_space=pl.ANY)
    big = pltpu.VMEM((16, 256, 128), F32)
    dma = pltpu.SemaphoreType.DMA
    cas = [jnp.asarray(table) for table in halves(cas_matrix())]
    columns = pl.pallas_call(
        kernel,
        name="hamiltonian",
        out_shape=jax.ShapeDtypeStruct((256, 16, 128), F32),
        in_specs=[vmem] * 6 + [anywhere] * 3,
        out_specs=anywhere,
        scratch_shapes=[
            pltpu.VMEM((2, 16, 64, GRID), F32),
            pltpu.VMEM((16, 64, GRID), F32),
            pltpu.VMEM((ENT, 8, 128), F32),
            pltpu.VMEM((256, 16, 128), F32),
            big,
            big,
            pltpu.VMEM((NPY, 16, 64, 128), F32),
            pltpu.VMEM((1024, 512), F32),
            pltpu.VMEM((NPY, 16, 64, 128), F32),
            big,
            big,
            pltpu.VMEM((1024, ENT), BF16),
            pltpu.VMEM((ENT, 1024), BF16),
            pltpu.VMEM((ENT, 128), F32),
            pltpu.VMEM((320, ENT), BF16),
            pltpu.VMEM((ENT, 512), F32),
            pltpu.VMEM((ENT, 512), BF16),
            pltpu.VMEM((ENT, 512), BF16),
            pltpu.VMEM((2, 5, 16, 128), F32),
            pltpu.VMEM((2, 5, 16, 128), F32),
            pltpu.VMEM((2, 5, 16, 128), F32),
            dma((3,)),
            dma((4,)),
            dma((4,)),
            dma((CHUNKS,)),
            dma((CHUNKS,)),
            dma((CHUNKS,)),
            dma,
            dma((2, 5)),
            dma((2, 5)),
            dma((2, 5)),
            dma((2, 5)),
        ],
        compiler_params=pltpu.CompilerParams(
            collective_id=0, has_side_effects=True, vmem_limit_bytes=56 * 2**20
        ),
    )(
        column_limit,
        entry_atom.reshape(1, ENT),
        entry_block.reshape(1, ENT),
        coupling,
        *cas,
        coefficients,
        potential,
        projectors,
    )
    whole = pl.BlockSpec((16, 64), lambda g: (0, 0))
    square = pl.BlockSpec((GRID, GRID), lambda g: (0, 0))
    bands = pl.BlockSpec((2, 8, 64, GRID), lambda g: (0, g, 0, 0))
    return pl.pallas_call(
        finish,
        name="finish",
        grid=(2,),
        out_shape=jax.ShapeDtypeStruct(coefficients.shape, F32),
        in_specs=[whole, square, square, pl.BlockSpec((256, 8, 128), lambda g: (0, g, 0)), bands],
        out_specs=bands,
        compiler_params=pltpu.CompilerParams(vmem_limit_bytes=60 * 2**20),
    )(column_limit, *cas, columns, coefficients)


def solution(mesh):
    in_specs = (
        P("band", "pz", "py", None),
        P("pz", "py", None),
        P("pz", "py"),
        P(("py", "pz"), None),
        P(("py", "pz")),
        P(("py", "pz"), None, None),
        P(),
    )
    out_specs = P("band", "pz", "py", None)
    return jax.shard_map(shards, mesh=mesh, in_specs=in_specs, out_specs=out_specs, check_vma=False)
```
